1024 devices in a mesh: blk: 256 (over z, x_hi, y), grp: 4 (over x_lo, core).
Axes of the slice: x: 8 (x_hi: 4, x_lo: 2; x = x_hi * 2 + x_lo), y: 8, z: 8, core: 2. Of those that a mesh axis runs over, the one named last changes fastest.
Arguments:
- queries: bfloat16 [131072, 4096], P(('blk', 'grp')), may hold values from -0.1875 to 0.1875
- passages: bfloat16 [2048, 4096], P(('blk', 'grp')), may hold values from -5 to 5
- pool: bfloat16 [131072, 4096], P(('blk', 'grp')), may hold values from -5 to 5
- positive_ids: int32 [131072], P(('blk', 'grp')), may hold values from 0 to 511
- request_lists: int32 [1024, 4, 32], P(('blk', 'grp')), may hold values from 0 to 127, as said below
- hard_refs: int32 [131072, 30], P(('blk', 'grp')), may hold values from 0 to 127, as said below
- hard_count: int32 [131072], P(('blk', 'grp')), may hold values from 1 to 30
Outputs:
- query_grad: bfloat16 [131072, 4096], P(('blk', 'grp'))
- query_loss: float32 [131072], P(('blk', 'grp'))
The draws below stay inside these ranges and needn't reach their ends.
Inputs may be any that keep to these rules, and one draw needn't show every extreme that they name: `request_lists`: entries of one list are distinct rows of that owner's 128 pool rows. `hard_refs`: the first hard_count entries of a row are distinct; later entries are padding and unused.
All inputs are finite; a program needn't handle non-finite values.
Results may differ from the reference program's by a relative error of at most 0.0034.
Values may be sent and summed in bfloat16 or wider, within the bound.
No kernel may reach another device: no remote copies, remote signals or barrier semaphores. Data moves between devices by JAX's collectives and lax.ppermute only.
A program may use at most 32 MiB of HBM per device.

```python
import math
import jax
import jax.numpy as jnp
from jax import lax

D = 4096
Q_DEV = 128
P_DEV = 2
POOL = 128
SLOTS = 32
HN_MAX = 30
QTOT = 131072
NPAS = 2048
NPOOL = 131072
N_BLK = 256
N_GRP = 4


def passage_base(key):
    base = jnp.clip(jax.random.normal(key, (NPAS, D), jnp.float32), -5.0, 5.0)
    base = base.at[0, 0].set(5.0)
    return base.at[1, 1].set(-5.0)


def draw_passages(key, part):
    shared = passage_base(key)
    return shared.astype(jnp.bfloat16)


def draw_queries(key, part):
    key = jax.random.fold_in(key, 11)
    spread = 3.0 / math.sqrt(D)
    base = jnp.clip(jax.random.normal(key, (QTOT, D), jnp.float32), -5.0, 5.0) * spread
    base = jnp.clip(base, -4.0 * spread, 4.0 * spread)
    base = base.at[0, 0].set(4.0 * spread)
    base = base.at[1, 0].set(-4.0 * spread)
    return base.astype(jnp.bfloat16)


def draw_request_lists(key, part):
    key = jax.random.fold_in(key, 37)
    list_keys = jax.random.split(key, N_BLK * N_GRP * N_GRP)
    lists = jax.vmap(lambda list_key: jax.random.permutation(list_key, POOL)[:SLOTS])(list_keys)
    return lists.reshape(N_BLK * N_GRP, N_GRP, SLOTS).astype(jnp.int32)


def draw_hard_refs(key, part):
    key = jax.random.fold_in(key, 23)
    row_keys = jax.random.split(key, QTOT)
    refs = jax.vmap(lambda row_key: jax.random.permutation(row_key, N_GRP * SLOTS)[:HN_MAX])(row_keys)
    return refs.astype(jnp.int32)


def draw_hard_count(key, part):
    key = jax.random.fold_in(key, 29)
    key_a, key_b, key_c = jax.random.split(key, 3)
    counts = jax.random.randint(key_a, (QTOT,), 1, HN_MAX + 1, jnp.int32)
    full_row = jax.random.randint(key_b, (), 0, QTOT, jnp.int32)
    short_row = (full_row + 1 + jax.random.randint(key_c, (), 0, QTOT - 1, jnp.int32)) % QTOT
    counts = counts.at[full_row].set(HN_MAX)
    counts = counts.at[short_row].set(1)
    return counts.astype(jnp.int32)


def touch_ends(values, stream_key, smallest, top_value):
    longest = values.shape.index(max(values.shape))
    spots = []
    for shift in (0, 1):
        where = [jax.random.randint(jax.random.fold_in(stream_key, axis), (), 0, length) for axis, length in enumerate(values.shape)]
        where[longest] = (where[longest] + shift) % values.shape[longest]
        spots.append(tuple(where))
    return values.at[spots[0]].set(smallest).at[spots[1]].set(top_value)


def block_scale(rng, dims, cuts, low, largest):
    factor_of, own = 1.0, jax.random.fold_in(rng, 6)
    for axis_at, blocks in cuts:
        steps = jnp.exp(jax.random.uniform(jax.random.fold_in(own, axis_at), (blocks,), jnp.float32, low / len(cuts), largest / len(cuts)))
        factor_of = factor_of * jnp.repeat(steps, dims[axis_at] // blocks).reshape([-1 if axis == axis_at else 1 for axis in range(len(dims))])
    return factor_of


def noise(key, shape, width, reach, pieces=(), kind=jnp.bfloat16):
    factor_of = block_scale(key, shape, pieces, -0.22, 0.18) if pieces else 1.0
    entries = jax.random.normal(key, shape, jnp.float32) * width * factor_of
    return jnp.minimum(jnp.maximum(entries, -reach), reach).astype(kind)


def setup_inputs(seed: int = 0) -> dict:
    arg_keys = jax.random.split(jax.random.key(seed), 8)
    queries = draw_queries(jax.random.fold_in(arg_keys[7], 71), 0)
    passages = draw_passages(jax.random.fold_in(arg_keys[7], 71), 0)
    pool = noise(arg_keys[2], (NPOOL, D), 1.0, 5.0, ((0, 1024),))
    positive_ids = touch_ends(jax.random.randint(arg_keys[3], (QTOT,), 0, P_DEV * N_BLK), jax.random.fold_in(arg_keys[3], 1), 0, (P_DEV * N_BLK) - 1).astype(jnp.int32)
    request_lists = draw_request_lists(jax.random.fold_in(arg_keys[7], 71), 0)
    hard_refs = draw_hard_refs(jax.random.fold_in(arg_keys[7], 71), 0)
    hard_count = draw_hard_count(jax.random.fold_in(arg_keys[7], 71), 0)
    return {"queries": queries, "passages": passages, "pool": pool, "positive_ids": positive_ids, "request_lists": request_lists, "hard_refs": hard_refs, "hard_count": hard_count}


def hard_mask(refs, count, span):
    table_iota = jnp.arange(span, dtype=jnp.int32)
    order = jnp.arange(refs.shape[1], dtype=jnp.int32)
    live = order[None, :] < count[:, None]
    hits = (refs[:, :, None] == table_iota[None, None, :]) & live[:, :, None]
    return jnp.sum(hits.astype(jnp.float32), axis=1)


def contrast(query_rows, cycle_rows, hard_table, positive, present):
    cycle_logits = jnp.dot(query_rows, cycle_rows.T, preferred_element_type=jnp.float32)
    hard_logits = jnp.dot(query_rows, hard_table.T, preferred_element_type=jnp.float32)
    hard_peak = jnp.max(jnp.where(present > 0, hard_logits, -jnp.inf), axis=1)
    peak_value = jnp.maximum(hard_peak, jnp.max(cycle_logits, axis=1))
    cycle_exp = jnp.exp(cycle_logits - peak_value[:, None])
    hard_exp = present * jnp.exp(hard_logits - peak_value[:, None])
    denominator = jnp.sum(cycle_exp, axis=1) + jnp.sum(hard_exp, axis=1)
    cycle_iota = jnp.arange(cycle_rows.shape[0], dtype=jnp.int32)
    onehot = (cycle_iota[None, :] == positive[:, None]).astype(jnp.float32)
    chosen = jnp.sum(cycle_logits * onehot, axis=1)
    query_loss = jnp.log(denominator) + peak_value - chosen
    cycle_weights = (cycle_exp / denominator[:, None] - onehot).astype(jnp.bfloat16)
    hard_weights = (hard_exp / denominator[:, None]).astype(jnp.bfloat16)
    summed = jnp.dot(cycle_weights, cycle_rows, preferred_element_type=jnp.float32)
    summed = summed + jnp.dot(hard_weights, hard_table, preferred_element_type=jnp.float32)
    return summed.astype(jnp.bfloat16), query_loss


def reference(queries, passages, pool, positive_ids, request_lists, hard_refs, hard_count):
    passage_grid = passages.reshape(N_BLK, N_GRP, P_DEV, D)
    pool_grid = pool.reshape(N_BLK, N_GRP, POOL, D)

    def device_work(device):
        blk_index = device // N_GRP
        grp_index = device % N_GRP
        cycle_rows = lax.dynamic_index_in_dim(passage_grid, grp_index, 1, keepdims=False).reshape(N_BLK * P_DEV, D)
        owner_pool = lax.dynamic_index_in_dim(pool_grid, blk_index, 0, keepdims=False)
        lists_here = lax.dynamic_index_in_dim(request_lists, device, 0, keepdims=False)
        hard_table = jax.vmap(lambda rows_of, picked_rows: rows_of[picked_rows])(owner_pool, lists_here)
        hard_table = hard_table.reshape(N_GRP * SLOTS, D)
        first_row = (device * Q_DEV).astype(jnp.int32)
        query_rows = lax.dynamic_slice_in_dim(queries, first_row, Q_DEV, 0)
        positive = lax.dynamic_slice_in_dim(positive_ids, first_row, Q_DEV, 0)
        refs_here = lax.dynamic_slice_in_dim(hard_refs, first_row, Q_DEV, 0)
        count_here = lax.dynamic_slice_in_dim(hard_count, first_row, Q_DEV, 0)
        present = hard_mask(refs_here, count_here, N_GRP * SLOTS)
        return contrast(query_rows, cycle_rows, hard_table, positive, present)

    grads, losses = lax.map(device_work, jnp.arange(N_BLK * N_GRP, dtype=jnp.int32))
    return grads.reshape(QTOT, D), losses.reshape(QTOT)
```

```python
import jax
import jax.numpy as jnp
from jax import lax
from jax.sharding import Mesh, PartitionSpec as P

AXES = ("z", "xh", "y", "xl", "c")
SIZES = (8, 4, 8, 2, 2)
WIDE = 3328


def hard_mask(refs, count, span):
    table_iota = jnp.arange(span, dtype=jnp.int32)
    order = jnp.arange(refs.shape[1], dtype=jnp.int32)
    live = order[None, :] < count[:, None]
    hits = (refs[:, :, None] == table_iota[None, None, :]) & live[:, :, None]
    return jnp.sum(hits.astype(jnp.float32), axis=1)


def spread(block, axes, members):
    copies = jnp.broadcast_to(block[None], (members,) + block.shape)
    return lax.all_to_all(copies, axes, 0, 0, tiled=True)


def dots(a, b):
    return lax.dot_general(a, b, (((1,), (1,)), ((), ())), preferred_element_type=jnp.float32)


def body(queries, passages, pool, positive_ids, request_lists, hard_refs, hard_count):
    depth = pool.shape[0]
    width = passages.shape[1]
    rest = width - WIDE
    slots = request_lists.shape[1] * request_lists.shape[2]

    with jax.named_scope("near_wide"):
        near_a = spread(passages[:, :WIDE], ("xh", "y"), 32).reshape(64, WIDE)
    with jax.named_scope("far_wide"):
        rows_a = lax.all_gather(near_a, "z", axis=0, tiled=True)
    tail, near_a = lax.optimization_barrier((passages[:, WIDE:], near_a))
    with jax.named_scope("near_rest"):
        near_b = spread(tail, ("z", "xh"), 32).reshape(64, rest)
    near_b, pool = lax.optimization_barrier((near_b, pool))
    with jax.named_scope("pool_x"):
        pool_x = lax.ppermute(pool, "xl", [(0, 1), (1, 0)])
        pool_c = lax.ppermute(pool, "c", [(0, 1), (1, 0)])
    with jax.named_scope("far_rest"):
        far_b = spread(near_b, "y", 8)
        rows_b = far_b.reshape(8, 32, 2, rest).transpose(1, 0, 2, 3).reshape(512, rest)
    with jax.named_scope("pool_xc"):
        pool_xc = lax.ppermute(pool_x, "c", [(0, 1), (1, 0)])

    with jax.named_scope("hard_logits"):
        present = hard_mask(hard_refs, hard_count, slots)
        xl, c = lax.axis_index("xl"), lax.axis_index("c")
        holders = jnp.stack([xl * 2 + c, xl * 2 + 1 - c, (1 - xl) * 2 + c, (1 - xl) * 2 + 1 - c])
        slot_owner = jnp.arange(slots, dtype=jnp.int32) // request_lists.shape[2]
        slot_row = request_lists.reshape(slots)
        place = jnp.arange(4 * depth, dtype=jnp.int32)
        match = (slot_owner[:, None] == jnp.repeat(holders, depth)[None, :]) & (
            slot_row[:, None] == (place % depth)[None, :]
        )
        present = jnp.dot(
            present.astype(jnp.bfloat16), match.astype(jnp.bfloat16), preferred_element_type=jnp.float32
        )
        pools = (pool, pool_c, pool_x, pool_xc)
        hard_logits = jnp.concatenate([dots(queries, p) for p in pools], axis=1)
        hard_peak = jnp.max(jnp.where(present > 0, hard_logits, -jnp.inf), axis=1)
    with jax.named_scope("cycle_logits"):
        logits_b = dots(queries[:, WIDE:], rows_b)
        cycle_logits = dots(queries[:, :WIDE], rows_a) + logits_b
        peak_value = jnp.maximum(hard_peak, jnp.max(cycle_logits, axis=1))
        cycle_exp = jnp.exp(cycle_logits - peak_value[:, None])
        hard_exp = jnp.where(present > 0, present * jnp.exp(hard_logits - peak_value[:, None]), 0.0)
        denominator = jnp.sum(cycle_exp, axis=1) + jnp.sum(hard_exp, axis=1)
        cycle_iota = jnp.arange(512, dtype=jnp.int32)
        onehot = (cycle_iota[None, :] == positive_ids[:, None]).astype(jnp.float32)
        chosen = jnp.sum(cycle_logits * onehot, axis=1)
    with jax.named_scope("gradient"):
        cycle_weights = (cycle_exp / denominator[:, None] - onehot).astype(jnp.bfloat16)
        hard_weights = (hard_exp / denominator[:, None]).astype(jnp.bfloat16)
        hard_part = sum(
            jnp.dot(hard_weights[:, i * depth : (i + 1) * depth], p, preferred_element_type=jnp.float32)
            for i, p in enumerate(pools)
        )
        part_a = jnp.dot(cycle_weights, rows_a, preferred_element_type=jnp.float32)
        part_b = jnp.dot(cycle_weights, rows_b, preferred_element_type=jnp.float32)
        gradient = jnp.concatenate([part_a + hard_part[:, :WIDE], part_b + hard_part[:, WIDE:]], axis=1)
        query_loss = jnp.log(denominator) + peak_value - chosen
    return (gradient.astype(jnp.bfloat16), query_loss)


def solution(mesh):
    grid = Mesh(mesh.devices.reshape(SIZES), AXES)
    return jax.shard_map(
        body,
        mesh=grid,
        in_specs=(
            P(AXES, None),
            P(AXES, None),
            P(AXES, None),
            P(AXES),
            P(AXES, None, None),
            P(AXES, None),
            P(AXES),
        ),
        out_specs=(P(AXES, None), P(AXES)),
        check_vma=False,
    )
```

```python
import jax
import jax.numpy as jnp
import numpy as np
from jax import lax
from jax.sharding import Mesh, PartitionSpec as P

DEVICES = np.arange(1024).reshape(8, 4, 8, 2, 2)


def lines(order):
    return DEVICES.transpose(order)


ALONG_Y = lines((0, 1, 3, 4, 2))
ALONG_Z = lines((1, 2, 3, 4, 0))
CROSS = lines((0, 2, 3, 1, 4)).reshape(-1, 8).tolist()
NEAR = np.concatenate([ALONG_Y[:, :, :, 0].reshape(-1, 8), ALONG_Z[:, :, :, 1].reshape(-1, 8)]).tolist()
FAR = np.concatenate([ALONG_Z[:, :, :, 0].reshape(-1, 8), ALONG_Y[:, :, :, 1].reshape(-1, 8)]).tolist()
OTHER_CORE = [(i, i ^ 1) for i in range(1024)]
OTHER_CHIP = [(i, i ^ 2) for i in range(1024)]


def hard_mask(refs, count, span):
    table_iota = jnp.arange(span, dtype=jnp.int32)
    order = jnp.arange(refs.shape[1], dtype=jnp.int32)
    live = order[None, :] < count[:, None]
    hits = (refs[:, :, None] == table_iota[None, None, :]) & live[:, :, None]
    return jnp.sum(hits.astype(jnp.float32), axis=1)


def dots(a, b):
    return lax.dot_general(a, b, (((1,), (1,)), ((), ())), preferred_element_type=jnp.float32)


def body(queries, passages, pool, positive_ids, request_lists, hard_refs, hard_count):
    depth = pool.shape[0]
    half = passages.shape[1] // 2
    slots = request_lists.shape[1] * request_lists.shape[2]
    device = lax.axis_index("d")
    core = device % 2
    chip = (device // 2) % 2

    with jax.named_scope("cross"):
        halves = passages.reshape(2, 2, half).transpose(1, 0, 2)
        sent = jnp.broadcast_to(halves[None], (4, 2, 2, half)).reshape(8, 2, half)
        got = lax.all_to_all(sent, "d", 0, 0, axis_index_groups=CROSS, tiled=True)
        got = got.reshape(4, 2, 2, half).transpose(1, 0, 2, 3).reshape(2, 8, half)
        got = jnp.where(core == 0, got, got[::-1])
    with jax.named_scope("near"):
        sent = jnp.broadcast_to(got.reshape(1, 16, half), (8, 16, half))
        near = lax.all_to_all(sent, "d", 0, 0, axis_index_groups=NEAR, tiled=True)
        near = near.reshape(8, 2, 8, half).transpose(1, 0, 2, 3).reshape(128, half)
    with jax.named_scope("far"):
        far = lax.all_gather(near, "d", axis_index_groups=FAR, axis=0, tiled=True).reshape(8, 2, 64, half)
    near, pool = lax.optimization_barrier((near, pool))
    with jax.named_scope("pools"):
        pool_x = lax.ppermute(pool, "d", OTHER_CHIP)
        pool_c = lax.ppermute(pool, "d", OTHER_CORE)
        pool_xc = lax.ppermute(pool_x, "d", OTHER_CORE)

    with jax.named_scope("hard_logits"):
        present = hard_mask(hard_refs, hard_count, slots)
        own = chip * 2 + core
        holders = jnp.stack([own, own ^ 1, own ^ 2, own ^ 3])
        slot_owner = jnp.arange(slots, dtype=jnp.int32) // request_lists.shape[2]
        slot_row = request_lists.reshape(slots)
        place = jnp.arange(4 * depth, dtype=jnp.int32)
        match = (slot_owner[:, None] == jnp.repeat(holders, depth)[None, :]) & (
            slot_row[:, None] == (place % depth)[None, :]
        )
        present = jnp.dot(
            present.astype(jnp.bfloat16), match.astype(jnp.bfloat16), preferred_element_type=jnp.float32
        )
        pools = (pool, pool_c, pool_x, pool_xc)
        hard_logits = jnp.concatenate([dots(queries, p) for p in pools], axis=1)
        hard_peak = jnp.max(jnp.where(present > 0, hard_logits, -jnp.inf), axis=1)

    far, hard_logits, present, hard_peak, pool_xc = lax.optimization_barrier(
        (far, hard_logits, present, hard_peak, pool_xc)
    )
    with jax.named_scope("swap"):
        swapped = far[:, 1].reshape(8, 8, 8, half).transpose(1, 0, 2, 3).reshape(512, half)
        swapped = lax.ppermute(swapped, "d", OTHER_CORE)
        rows_own = far[:, 0].reshape(512, half)
    with jax.named_scope("cycle_logits"):
        queries_own = lax.dynamic_slice_in_dim(queries, core * half, half, 1)
        queries_swap = lax.dynamic_slice_in_dim(queries, (1 - core) * half, half, 1)
        cycle_logits = dots(queries_own, rows_own) + dots(queries_swap, swapped)
        peak_value = jnp.maximum(hard_peak, jnp.max(cycle_logits, axis=1))
        cycle_exp = jnp.exp(cycle_logits - peak_value[:, None])
        hard_exp = jnp.where(present > 0, present * jnp.exp(hard_logits - peak_value[:, None]), 0.0)
        denominator = jnp.sum(cycle_exp, axis=1) + jnp.sum(hard_exp, axis=1)
        place = jnp.arange(512, dtype=jnp.int32)
        outer, inner, hi, row = place // 64, (place // 8) % 8, (place // 2) % 4, place % 2
        far_z, far_y = jnp.where(core == 0, outer, inner), jnp.where(core == 0, inner, outer)
        index = ((far_z * 4 + hi) * 8 + far_y) * 2 + row
        onehot = (index[None, :] == positive_ids[:, None]).astype(jnp.float32)
        chosen = jnp.sum(cycle_logits * onehot, axis=1)
    with jax.named_scope("gradient"):
        cycle_weights = (cycle_exp / denominator[:, None] - onehot).astype(jnp.bfloat16)
        hard_weights = (hard_exp / denominator[:, None]).astype(jnp.bfloat16)
        hard_part = sum(
            jnp.dot(hard_weights[:, i * depth : (i + 1) * depth], p, preferred_element_type=jnp.float32)
            for i, p in enumerate((pool, pool_c, pool_x, pool_xc))
        )
        part_own = jnp.dot(cycle_weights, rows_own, preferred_element_type=jnp.float32)
        part_swap = jnp.dot(cycle_weights, swapped, preferred_element_type=jnp.float32)
        low = jnp.where(core == 0, part_own, part_swap)
        high = jnp.where(core == 0, part_swap, part_own)
        gradient = jnp.concatenate([low, high], axis=1) + hard_part
        query_loss = jnp.log(denominator) + peak_value - chosen
    return (gradient.astype(jnp.bfloat16), query_loss)


def solution(mesh):
    flat = Mesh(mesh.devices.reshape(1024), ("d",))
    return jax.shard_map(
        body,
        mesh=flat,
        in_specs=(P("d", None), P("d", None), P("d", None), P("d"), P("d", None, None), P("d", None), P("d")),
        out_specs=(P("d", None), P("d")),
        check_vma=False,
    )
```

```python
import functools

import jax
import jax.numpy as jnp
import numpy as np
from jax import lax
from jax.experimental import pallas as pl
from jax.experimental.pallas import tpu as pltpu
from jax.sharding import Mesh, PartitionSpec as P

DEVICES = np.arange(1024).reshape(8, 4, 8, 2, 2)


def lines(order):
    return DEVICES.transpose(order)


ALONG_Y = lines((0, 1, 3, 4, 2))
ALONG_Z = lines((1, 2, 3, 4, 0))
CROSS = lines((0, 2, 3, 1, 4)).reshape(-1, 8).tolist()
NEAR = np.concatenate([ALONG_Y[:, :, :, 0].reshape(-1, 8), ALONG_Z[:, :, :, 1].reshape(-1, 8)]).tolist()
RINGS = np.concatenate([ALONG_Z[:, :, :, 0].reshape(-1, 8), ALONG_Y[:, :, :, 1].reshape(-1, 8)]).tolist()
UP = [(g[i], g[(i + 1) % 8]) for g in RINGS for i in range(8)]
DOWN = [(g[i], g[i - 1]) for g in RINGS for i in range(8)]
DOWN_OTHER_CORE = [(a, b ^ 1) for a, b in DOWN]
OTHER_CORE = [(i, i ^ 1) for i in range(1024)]
OTHER_CHIP = [(i, i ^ 2) for i in range(1024)]
BLOCK = 64


def dots(a, b):
    return lax.dot_general(a, b, (((1,), (1,)), ((), ())), preferred_element_type=jnp.float32)


def hard_kernel(place_ref, refs_ref, count_ref, list_ref, q_ref, p0, p1, p2, p3, out_ref):
    rows, most = refs_ref.shape
    span = list_ref.shape[0]
    slots = span // 4
    own = place_ref[3]
    column = lax.broadcasted_iota(jnp.int32, (rows, span), 1)
    refs = refs_ref[...]
    live = lax.broadcasted_iota(jnp.int32, refs.shape, 1) < count_ref[...]
    refs = jnp.where(live, refs, -1)
    present = jnp.zeros((rows, span), jnp.float32)
    for i in range(most):
        present = present + jnp.where(refs[:, i : i + 1] == column, 1.0, 0.0)
    present = present.astype(jnp.bfloat16)
    slot = lax.broadcasted_iota(jnp.int32, (span, span), 0)
    row = lax.broadcasted_iota(jnp.int32, (span, span), 1)
    same = list_ref[...] == row
    for i, pool in enumerate((p0, p1, p2, p3)):
        match = jnp.where(same & (lax.div(slot, slots) == (own ^ i)), 1.0, 0.0).astype(jnp.bfloat16)
        used = jnp.dot(present, match, preferred_element_type=jnp.float32)
        out_ref[:, i * span : (i + 1) * span] = jnp.where(used > 0, dots(q_ref[...], pool[...]), -jnp.inf)


def passage(shape, dim, place, ring_is_z):
    at = lax.broadcasted_iota(jnp.int32, shape, dim)
    block, inner, hi, row = at >> 6, (at >> 3) & 7, (at >> 1) & 3, at & 1
    step = (block + 1) >> 1
    shift = jnp.where((block & 1) == 1, 8 - step, step)
    ring_z, ring_y = (place[0] + shift) & 7, (place[1] + shift) & 7
    z = jnp.where(ring_is_z, ring_z, inner)
    y = jnp.where(ring_is_z, inner, ring_y)
    return ((z * 4 + hi) * 8 + y) * 2 + row


def tail_kernel(place_ref, pos_ref, hard_ref, q_ref, *rest):
    blocks, (p0, p1, p2, p3), (grad_ref, loss_ref, own_ref, swap_ref) = rest[:13], rest[13:17], rest[17:]
    near, l1, r1, l2, r2, l3, r3, last, cnear, c1, c2, c3, clast = blocks
    core = place_ref[2]
    half = own_ref.shape[1]
    total = own_ref.shape[0]
    for i, part in enumerate((near, l1, r1, l2, r2, l3, r3)):
        own_ref[i * BLOCK : (i + 1) * BLOCK, :] = part[0]
    own_ref[7 * BLOCK :, :] = last[...]
    swap_ref[:BLOCK, :] = cnear[...]
    for i, part in enumerate((c1, c2, c3)):
        for j in range(2):
            at = (2 * i + j + 1) * BLOCK
            swap_ref[at : at + BLOCK, :] = part[j]
    swap_ref[7 * BLOCK :, :] = clast[...]

    place = (place_ref[0], place_ref[1])
    q_own = q_ref[:, pl.ds(pl.multiple_of(core * half, 128), half)]
    q_swap = q_ref[:, pl.ds(pl.multiple_of((1 - core) * half, 128), half)]
    own_index = passage((1, total), 1, place, core == 0)
    swap_index = passage((total, 1), 0, place, core == 1)
    order = jnp.where(swap_index == own_index, 1.0, 0.0).astype(jnp.bfloat16)
    swap_logits = dots(q_swap, swap_ref[...])
    high = swap_logits.astype(jnp.bfloat16)
    left = swap_logits - high.astype(jnp.float32)
    middle = left.astype(jnp.bfloat16)
    low = (left - middle.astype(jnp.float32)).astype(jnp.bfloat16)
    moved = jnp.dot(low, order, preferred_element_type=jnp.float32)
    moved = moved + jnp.dot(middle, order, preferred_element_type=jnp.float32)
    moved = moved + jnp.dot(high, order, preferred_element_type=jnp.float32)
    logits = dots(q_own, own_ref[...]) + moved

    hard = hard_ref[...]
    peak = jnp.maximum(jnp.max(logits, axis=1, keepdims=True), jnp.max(hard, axis=1, keepdims=True))
    cycle_exp = jnp.exp(logits - peak)
    hard_exp = jnp.exp(hard - peak)
    denominator = jnp.sum(cycle_exp, axis=1, keepdims=True) + jnp.sum(hard_exp, axis=1, keepdims=True)
    positive = own_index == pos_ref[...]
    chosen = jnp.sum(jnp.where(positive, logits, 0.0), axis=1, keepdims=True)
    loss_ref[...] = jnp.log(denominator) + peak - chosen
    weights = (cycle_exp / denominator - jnp.where(positive, 1.0, 0.0)).astype(jnp.bfloat16)
    hard_weights = (hard_exp / denominator).astype(jnp.bfloat16)
    swap_weights = dots(weights, order).astype(jnp.bfloat16)

    depth = p0.shape[0]
    for mine, w, rows in ((core, weights, own_ref), (1 - core, swap_weights, swap_ref)):
        for chunk in range(0, half, 512):
            at = pl.ds(pl.multiple_of(mine * half + chunk, 128), 512)
            total_grad = jnp.dot(w, rows[:, chunk : chunk + 512], preferred_element_type=jnp.float32)
            for i, pool in enumerate((p0, p1, p2, p3)):
                part = hard_weights[:, i * depth : (i + 1) * depth]
                total_grad += jnp.dot(part, pool[:, at], preferred_element_type=jnp.float32)
            grad_ref[:, at] = total_grad.astype(jnp.bfloat16)


VMEM = functools.partial(pl.BlockSpec, memory_space=pltpu.VMEM)
SMEM = functools.partial(pl.BlockSpec, memory_space=pltpu.SMEM)


def hard_call(place, refs, count, lists, queries, pools):
    rows = queries.shape[0]
    span = lists.size
    return pl.pallas_call(
        hard_kernel,
        out_shape=jax.ShapeDtypeStruct((rows, 4 * span), jnp.float32),
        in_specs=[SMEM()] + [VMEM()] * 8,
        out_specs=VMEM(),
        compiler_params=pltpu.CompilerParams(vmem_limit_bytes=8 * 2**20),
        cost_estimate=pl.CostEstimate(flops=2**29, bytes_accessed=6 * 2**20, transcendentals=0),
        name="hard",
    )(place, refs, count.reshape(rows, 1), lists.reshape(span, 1), queries, *pools)


def tail_call(place, positive, hard, queries, blocks, pools):
    rows, width = queries.shape
    half = width // 2
    return pl.pallas_call(
        tail_kernel,
        out_shape=(
            jax.ShapeDtypeStruct((rows, width), jnp.bfloat16),
            jax.ShapeDtypeStruct((rows, 1), jnp.float32),
        ),
        in_specs=[SMEM()] + [VMEM()] * (3 + len(blocks) + len(pools)),
        out_specs=(VMEM(), VMEM()),
        scratch_shapes=[pltpu.VMEM((8 * BLOCK, half), jnp.bfloat16), pltpu.VMEM((8 * BLOCK, half), jnp.bfloat16)],
        compiler_params=pltpu.CompilerParams(vmem_limit_bytes=16 * 2**20),
        cost_estimate=pl.CostEstimate(flops=2**31, bytes_accessed=12 * 2**20, transcendentals=2**17),
        name="tail",
    )(place, positive.reshape(rows, 1), hard, queries, *blocks, *pools)


def body(queries, passages, pool, positive_ids, request_lists, hard_refs, hard_count):
    half = passages.shape[1] // 2
    device = lax.axis_index("d")
    core = device & 1
    place = jnp.stack([device >> 7, (device >> 2) & 7, core, device & 3]).astype(jnp.int32)

    with jax.named_scope("cross"):
        halves = passages.reshape(2, 2, half).transpose(1, 0, 2)
        sent = jnp.broadcast_to(halves[None], (4, 2, 2, half)).reshape(8, 2, half)
        got = lax.all_to_all(sent, "d", 0, 0, axis_index_groups=CROSS, tiled=True)
        got = got.reshape(4, 2, 2, half).transpose(1, 0, 2, 3).reshape(2, 8, half)
        got = jnp.where(core == 0, got, got[::-1])
    with jax.named_scope("near"):
        sent = jnp.broadcast_to(got.reshape(1, 16, half), (8, 16, half))
        near = lax.all_to_all(sent, "d", 0, 0, axis_index_groups=NEAR, tiled=True)
        near = near.reshape(8, 2, 8, half).transpose(1, 0, 2, 3).reshape(2, BLOCK, half)
    with jax.named_scope("ring"):
        up, down, handed = near, near, [lax.ppermute(near[1], "d", OTHER_CORE)]
        own = [near]
        for _ in range(3):
            up, down = lax.ppermute(up, "d", UP), lax.ppermute(down, "d", DOWN)
            own += [up, down]
            handed.append(lax.ppermute(jnp.stack([up[1], down[1]]), "d", OTHER_CORE))
        own.append(lax.ppermute(up[0], "d", UP))
        handed.append(lax.ppermute(down[1], "d", DOWN_OTHER_CORE))
    with jax.named_scope("pools"):
        near, pool = lax.optimization_barrier((near, pool))
        pool_x = lax.ppermute(pool, "d", OTHER_CHIP)
        pool_c = lax.ppermute(pool, "d", OTHER_CORE)
        pool_xc = lax.ppermute(pool_x, "d", OTHER_CORE)
        pools = (pool, pool_c, pool_x, pool_xc)
    hard = hard_call(place, hard_refs, hard_count, request_lists, queries, pools)
    grad, loss = tail_call(place, positive_ids, hard, queries, own + handed, pools)
    return grad, loss.reshape(-1)


def solution(mesh):
    flat = Mesh(mesh.devices.reshape(1024), ("d",))
    return jax.shard_map(
        body,
        mesh=flat,
        in_specs=(P("d", None), P("d", None), P("d", None), P("d"), P("d", None, None), P("d", None), P("d")),
        out_specs=(P("d", None), P("d")),
        check_vma=False,
    )
```

```python
import functools

import jax
import jax.numpy as jnp
import numpy as np
from jax import lax
from jax.experimental import pallas as pl
from jax.experimental.pallas import tpu as pltpu
from jax.sharding import Mesh, PartitionSpec as P

DEVICES = np.arange(1024).reshape(8, 4, 8, 2, 2)


def lines(order):
    return DEVICES.transpose(order)


ALONG_Y = lines((0, 1, 3, 4, 2))
ALONG_Z = lines((1, 2, 3, 4, 0))
CROSS = lines((0, 2, 3, 1, 4)).reshape(-1, 8).tolist()
NEAR = np.concatenate([ALONG_Y[:, :, :, 0].reshape(-1, 8), ALONG_Z[:, :, :, 1].reshape(-1, 8)]).tolist()
RINGS = np.concatenate([ALONG_Z[:, :, :, 0].reshape(-1, 8), ALONG_Y[:, :, :, 1].reshape(-1, 8)]).tolist()
UP = [(g[i], g[(i + 1) % 8]) for g in RINGS for i in range(8)]
DOWN = [(g[i], g[i - 1]) for g in RINGS for i in range(8)]
DOWN_OTHER_CORE = [(a, b ^ 1) for a, b in DOWN]
OTHER_CORE = [(i, i ^ 1) for i in range(1024)]
OTHER_CHIP = [(i, i ^ 2) for i in range(1024)]
BLOCK = 64


def dots(a, b):
    return lax.dot_general(a, b, (((1,), (1,)), ((), ())), preferred_element_type=jnp.float32)


def hard_kernel(place_ref, refs_ref, count_ref, list_ref, q_ref, p0, p1, p2, p3, out_ref):
    most, rows = refs_ref.shape
    owners, slots = list_ref.shape
    span = owners * slots
    own = place_ref[3]
    at = lax.broadcasted_iota(jnp.int32, (span, rows), 0)
    live = lax.broadcasted_iota(jnp.int32, (most, rows), 0) < count_ref[...]
    refs = jnp.where(live, refs_ref[...], -1)
    present = jnp.zeros((span, rows), jnp.float32)
    for i in range(most):
        present = present + jnp.where(refs[i : i + 1, :] == at, 1.0, 0.0)
    present = present.astype(jnp.bfloat16)
    row = lax.broadcasted_iota(jnp.int32, (span, span), 0)
    owner = lax.broadcasted_iota(jnp.int32, (span, span), 1) // slots
    lists = jnp.concatenate([list_ref[i : i + 1, :] for i in range(owners)], axis=1)
    same = lists == row
    for i, pool in enumerate((p0, p1, p2, p3)):
        match = jnp.where(same & (owner == (own ^ i)), 1.0, 0.0).astype(jnp.bfloat16)
        used = lax.dot_general(present, match, (((0,), (1,)), ((), ())), preferred_element_type=jnp.float32)
        out_ref[:, i * span : (i + 1) * span] = jnp.where(used > 0, dots(q_ref[...], pool[...]), -jnp.inf)


def passage(shape, dim, place, ring_is_z):
    at = lax.broadcasted_iota(jnp.int32, shape, dim)
    block, inner, hi, row = at >> 6, (at >> 3) & 7, (at >> 1) & 3, at & 1
    step = (block + 1) >> 1
    shift = jnp.where((block & 1) == 1, 8 - step, step)
    ring_z, ring_y = (place[0] + shift) & 7, (place[1] + shift) & 7
    z = jnp.where(ring_is_z, ring_z, inner)
    y = jnp.where(ring_is_z, inner, ring_y)
    return ((z * 4 + hi) * 8 + y) * 2 + row


def hand_kernel(*refs):
    (keep_ref, give_ref), blocks = refs[-2:], refs[:-2]
    for i, block in enumerate(blocks):
        keep_ref[i] = block[0]
        give_ref[i] = block[1]


def tail_kernel(place_ref, pos_ref, hard_ref, q_ref, *rest):
    blocks, (p0, p1, p2, p3), (grad_ref, loss_ref, own_ref, swap_ref) = rest[:8], rest[8:12], rest[12:]
    core = place_ref[2]
    half = own_ref.shape[1]
    total = own_ref.shape[0]
    for parts, rows_ref in ((blocks[:4], own_ref), (blocks[4:], swap_ref)):
        at = 0
        for part in parts:
            for i in range(part.shape[0]):
                rows_ref[at : at + BLOCK, :] = part[i]
                at += BLOCK

    place = (place_ref[0], place_ref[1])
    q_own = q_ref[:, pl.ds(pl.multiple_of(core * half, 128), half)]
    q_swap = q_ref[:, pl.ds(pl.multiple_of((1 - core) * half, 128), half)]
    own_index = passage((1, total), 1, place, core == 0)
    swap_index = passage((total, 1), 0, place, core == 1)
    order = jnp.where(swap_index == own_index, 1.0, 0.0).astype(jnp.bfloat16)
    swap_logits = dots(q_swap, swap_ref[...])
    high = swap_logits.astype(jnp.bfloat16)
    left = swap_logits - high.astype(jnp.float32)
    middle = left.astype(jnp.bfloat16)
    low = (left - middle.astype(jnp.float32)).astype(jnp.bfloat16)
    moved = jnp.dot(low, order, preferred_element_type=jnp.float32)
    moved = moved + jnp.dot(middle, order, preferred_element_type=jnp.float32)
    moved = moved + jnp.dot(high, order, preferred_element_type=jnp.float32)
    logits = dots(q_own, own_ref[...]) + moved

    hard = hard_ref[...]
    peak = jnp.maximum(jnp.max(logits, axis=1, keepdims=True), jnp.max(hard, axis=1, keepdims=True))
    cycle_exp = jnp.exp(logits - peak)
    hard_exp = jnp.exp(hard - peak)
    denominator = jnp.sum(cycle_exp, axis=1, keepdims=True) + jnp.sum(hard_exp, axis=1, keepdims=True)
    rows = q_ref.shape[0]
    eye = lax.broadcasted_iota(jnp.int32, (rows, rows), 0) == lax.broadcasted_iota(jnp.int32, (rows, rows), 1)
    positives = jnp.sum(jnp.where(eye, pos_ref[...].astype(jnp.float32), 0.0), axis=1, keepdims=True)
    positive = own_index == positives.astype(jnp.int32)
    chosen = jnp.sum(jnp.where(positive, logits, 0.0), axis=1, keepdims=True)
    loss = jnp.log(denominator) + peak - chosen
    loss_ref[...] = jnp.sum(jnp.where(eye, loss, 0.0), axis=0, keepdims=True)
    weights = (cycle_exp / denominator - jnp.where(positive, 1.0, 0.0)).astype(jnp.bfloat16)
    hard_weights = (hard_exp / denominator).astype(jnp.bfloat16)
    swap_weights = dots(weights, order).astype(jnp.bfloat16)

    for mine, w, rows_ref in ((core, weights, own_ref), (1 - core, swap_weights, swap_ref)):
        all_weights = jnp.concatenate([w, hard_weights], axis=1)
        for chunk in range(0, half, 512):
            at = pl.ds(pl.multiple_of(mine * half + chunk, 128), 512)
            all_rows = [rows_ref[:, chunk : chunk + 512]] + [pool[:, at] for pool in (p0, p1, p2, p3)]
            grad = jnp.dot(all_weights, jnp.concatenate(all_rows, axis=0), preferred_element_type=jnp.float32)
            grad_ref[:, at] = grad.astype(jnp.bfloat16)


VMEM = functools.partial(pl.BlockSpec, memory_space=pltpu.VMEM)
SMEM = functools.partial(pl.BlockSpec, memory_space=pltpu.SMEM)


def hard_call(place, refs, count, lists, queries, pools):
    rows = queries.shape[0]
    span = lists.size
    refs, count = refs.T, count.reshape(1, rows)
    return pl.pallas_call(
        hard_kernel,
        out_shape=jax.ShapeDtypeStruct((rows, 4 * span), jnp.float32),
        in_specs=[SMEM()] + [VMEM()] * 8,
        out_specs=VMEM(),
        compiler_params=pltpu.CompilerParams(vmem_limit_bytes=8 * 2**20),
        cost_estimate=pl.CostEstimate(flops=2**33, bytes_accessed=6 * 2**20, transcendentals=0),
        name="hard",
    )(place, refs, count, lists[0], queries, *pools)


def hand_call(*blocks):
    out = jax.ShapeDtypeStruct((len(blocks),) + blocks[0].shape[1:], blocks[0].dtype)
    return pl.pallas_call(
        hand_kernel,
        out_shape=(out, out),
        in_specs=[VMEM()] * len(blocks),
        out_specs=(VMEM(), VMEM()),
        compiler_params=pltpu.CompilerParams(vmem_limit_bytes=8 * 2**20),
        cost_estimate=pl.CostEstimate(flops=2**33, bytes_accessed=4 * 2**20, transcendentals=0),
        name="hand",
    )(*blocks)


def tail_call(place, positive, hard, queries, blocks, pools):
    rows, width = queries.shape
    half = width // 2
    return pl.pallas_call(
        tail_kernel,
        out_shape=(
            jax.ShapeDtypeStruct((rows, width), jnp.bfloat16),
            jax.ShapeDtypeStruct((1, rows), jnp.float32),
        ),
        in_specs=[SMEM()] + [VMEM()] * (3 + len(blocks) + len(pools)),
        out_specs=(VMEM(), VMEM()),
        scratch_shapes=[pltpu.VMEM((8 * BLOCK, half), jnp.bfloat16), pltpu.VMEM((8 * BLOCK, half), jnp.bfloat16)],
        compiler_params=pltpu.CompilerParams(vmem_limit_bytes=16 * 2**20),
        cost_estimate=pl.CostEstimate(flops=2**31, bytes_accessed=12 * 2**20, transcendentals=2**17),
        name="tail",
    )(place, positive.reshape(1, rows), hard, queries, *blocks, *pools)


def body(queries, passages, pool, positive_ids, request_lists, hard_refs, hard_count):
    half = passages.shape[1] // 2
    device = lax.axis_index("d")
    core = device & 1
    place = jnp.stack([device >> 7, (device >> 2) & 7, core, device & 3]).astype(jnp.int32)

    with jax.named_scope("cross"):
        halves = passages.reshape(2, 2, half).transpose(1, 0, 2)
        sent = jnp.broadcast_to(halves[None], (4, 2, 2, half)).reshape(8, 2, half)
        got = lax.all_to_all(sent, "d", 0, 0, axis_index_groups=CROSS, tiled=True)
        got = got.reshape(4, 2, 2, half).transpose(1, 0, 2, 3).reshape(2, 8, half)
        got = jnp.where(core == 0, got, got[::-1])
    with jax.named_scope("near"):
        sent = jnp.broadcast_to(got.reshape(1, 16, half), (8, 16, half))
        near = lax.all_to_all(sent, "d", 0, 0, axis_index_groups=NEAR, tiled=True)
        near = near.reshape(8, 2, 8, half).transpose(1, 0, 2, 3).reshape(2, BLOCK, half)
    with jax.named_scope("ring"):
        up, down, held, kept, handed = near, near, [near], [], []
        for step in range(3):
            up, down = lax.ppermute(up, "d", UP), lax.ppermute(down, "d", DOWN)
            if step == 2:
                up, down, *handed = lax.optimization_barrier((up, down, *handed))
            keep, give = hand_call(*held, up, down)
            kept.append(keep)
            handed.append(lax.ppermute(give, "d", OTHER_CORE))
            held = []
        kept.append(lax.ppermute(up[:1], "d", UP))
        handed.append(lax.ppermute(down[1:], "d", DOWN_OTHER_CORE))
    with jax.named_scope("pools"):
        near, pool = lax.optimization_barrier((near, pool))
        pool_x = lax.ppermute(pool, "d", OTHER_CHIP)
        pool_c = lax.ppermute(pool, "d", OTHER_CORE)
        pool_xc = lax.ppermute(pool_x, "d", OTHER_CORE)
        pools = (pool, pool_c, pool_x, pool_xc)
    hard = hard_call(place, hard_refs, hard_count, request_lists, queries, pools)
    grad, loss = tail_call(place, positive_ids, hard, queries, kept + handed, pools)
    return grad, loss.reshape(-1)


def solution(mesh):
    flat = Mesh(mesh.devices.reshape(1024), ("d",))
    return jax.shard_map(
        body,
        mesh=flat,
        in_specs=(P("d", None), P("d", None), P("d", None), P("d"), P("d", None, None), P("d", None), P("d")),
        out_specs=(P("d", None), P("d")),
        check_vma=False,
    )
```

```python
import functools

import jax
import jax.numpy as jnp
import numpy as np
from jax import lax
from jax.experimental import pallas as pl
from jax.experimental.pallas import tpu as pltpu
from jax.sharding import Mesh, PartitionSpec as P

DEVICES = np.arange(1024).reshape(8, 4, 8, 2, 2)


def lines(order):
    return DEVICES.transpose(order)


ALONG_Y = lines((0, 1, 3, 4, 2))
ALONG_Z = lines((1, 2, 3, 4, 0))
CROSS = lines((0, 2, 3, 1, 4)).reshape(-1, 8).tolist()
NEAR = np.concatenate([ALONG_Y[:, :, :, 0].reshape(-1, 8), ALONG_Z[:, :, :, 1].reshape(-1, 8)]).tolist()


def ring(groups):
    return [(g[i], g[(i + 1 - 2 * (g[i] & 1)) % 8]) for g in groups.reshape(-1, 8) for i in range(8)]


RING_Z = ring(ALONG_Z)
RING_Y = ring(ALONG_Y)
OTHER_CORE = [(i, i ^ 1) for i in range(1024)]
OTHER_CHIP = [(i, i ^ 2) for i in range(1024)]
BLOCK = 64


def dots(a, b):
    return lax.dot_general(a, b, (((1,), (1,)), ((), ())), preferred_element_type=jnp.float32)


def hard_kernel(place_ref, refs_ref, count_ref, list_ref, q_ref, pool, out_ref):
    most, rows = refs_ref.shape
    owners, slots = list_ref.shape
    span = owners * slots
    own = place_ref[3]
    at = lax.broadcasted_iota(jnp.int32, (span, rows), 0)
    live = lax.broadcasted_iota(jnp.int32, (most, rows), 0) < count_ref[...]
    refs = jnp.where(live, refs_ref[...], -1)
    present = jnp.zeros((span, rows), jnp.float32)
    for i in range(most):
        present = present + jnp.where(refs[i : i + 1, :] == at, 1.0, 0.0)
    present = present.astype(jnp.bfloat16)
    row = lax.broadcasted_iota(jnp.int32, (span, span), 0)
    owner = lax.broadcasted_iota(jnp.int32, (span, span), 1) // slots
    lists = jnp.concatenate([list_ref[i : i + 1, :] for i in range(owners)], axis=1)
    same = lists == row
    for i in range(4):
        match = jnp.where(same & (owner == (own ^ i)), 1.0, 0.0).astype(jnp.bfloat16)
        used = lax.dot_general(present, match, (((0,), (1,)), ((), ())), preferred_element_type=jnp.float32)
        value = 0.0 if i else dots(q_ref[...], pool[...])
        out_ref[:, i * span : (i + 1) * span] = jnp.where(used > 0, value, -jnp.inf)


def hard_rest_kernel(hard_ref, q_ref, p1, p2, p3, out_ref):
    span = p1.shape[0]
    out_ref[:, :span] = hard_ref[:, :span]
    for i, pool in ((1, p1), (2, p2), (3, p3)):
        at = slice(i * span, (i + 1) * span)
        out_ref[:, at] = hard_ref[:, at] + dots(q_ref[...], pool[...])


def passage(shape, dim, place, ring_is_z):
    at = lax.broadcasted_iota(jnp.int32, shape, dim)
    block, inner, hi, row = at >> 6, (at >> 3) & 7, (at >> 1) & 3, at & 1
    step = (block + 1) >> 1
    below = (block & 1) != place[2]
    shift = jnp.where(below, 8 - step, step)
    if ring_is_z:
        z, y = (place[0] + shift) & 7, inner
    else:
        z, y = inner, (place[1] + shift) & 7
    return ((z * 4 + hi) * 8 + y) * 2 + row


def sort_kernel(place_ref, mine_ref, theirs_ref, left_ref, right_ref, keep_ref):
    core = place_ref[2]
    own = 8 * core

    def order(source, target):
        for i in range(8):
            piece = source[i]
            first, second = piece[:8], piece[8:]
            at = slice(8 * i, 8 * i + 8)
            target[0, at] = jnp.where(own == 0, first, second)
            target[1, at] = jnp.where(own == 0, second, first)

    @pl.when(core == 0)
    def _():
        order(mine_ref, left_ref)
        order(theirs_ref, right_ref)

    @pl.when(core == 1)
    def _():
        order(theirs_ref, left_ref)
        order(mine_ref, right_ref)

    keep_ref[0] = left_ref[0]
    keep_ref[1] = right_ref[0]


def hand_kernel(left_ref, right_ref, keep_left_ref, keep_right_ref, give_ref):
    keep_left_ref[0] = left_ref[0]
    keep_right_ref[0] = right_ref[0]
    give_ref[0] = left_ref[1]
    give_ref[1] = right_ref[1]


def tail_kernel(place_ref, pos_ref, hard_ref, q_ref, *rest):
    blocks, (p0, p1, p2, p3), (grad_ref, loss_ref, left_ref, right_ref) = rest[:12], rest[12:16], rest[16:]
    keep, l1, r1, e1, l2, r2, e2, l3, r3, e3, l4, r4 = blocks
    half = left_ref.shape[1]
    total = left_ref.shape[0]
    lefts = (keep.at[0], l1.at[0], e1.at[0], l2.at[0], e2.at[0], l3.at[0], e3.at[0], l4.at[0])
    rights = (keep.at[1], r1.at[0], e1.at[1], r2.at[0], e2.at[1], r3.at[0], e3.at[1], r4.at[0])
    for parts, rows_ref in ((lefts, left_ref), (rights, right_ref)):
        for i, part in enumerate(parts):
            rows_ref[i * BLOCK : (i + 1) * BLOCK, :] = part[...]

    place = (place_ref[0], place_ref[1], place_ref[2])
    left_index = passage((1, total), 1, place, True)
    right_index = passage((total, 1), 0, place, False)
    order = jnp.where(right_index == left_index, 1.0, 0.0).astype(jnp.bfloat16)
    right_logits = dots(q_ref[:, half:], right_ref[...])
    high = right_logits.astype(jnp.bfloat16)
    left_over = right_logits - high.astype(jnp.float32)
    middle = left_over.astype(jnp.bfloat16)
    low = (left_over - middle.astype(jnp.float32)).astype(jnp.bfloat16)
    moved = jnp.dot(low, order, preferred_element_type=jnp.float32)
    moved = moved + jnp.dot(middle, order, preferred_element_type=jnp.float32)
    moved = moved + jnp.dot(high, order, preferred_element_type=jnp.float32)
    logits = dots(q_ref[:, :half], left_ref[...]) + moved

    hard = hard_ref[...]
    peak = jnp.maximum(jnp.max(logits, axis=1, keepdims=True), jnp.max(hard, axis=1, keepdims=True))
    cycle_exp = jnp.exp(logits - peak)
    hard_exp = jnp.exp(hard - peak)
    denominator = jnp.sum(cycle_exp, axis=1, keepdims=True) + jnp.sum(hard_exp, axis=1, keepdims=True)
    rows = q_ref.shape[0]
    eye = lax.broadcasted_iota(jnp.int32, (rows, rows), 0) == lax.broadcasted_iota(jnp.int32, (rows, rows), 1)
    positives = jnp.sum(jnp.where(eye, pos_ref[...].astype(jnp.float32), 0.0), axis=1, keepdims=True)
    positive = left_index == positives.astype(jnp.int32)
    chosen = jnp.sum(jnp.where(positive, logits, 0.0), axis=1, keepdims=True)
    loss = jnp.log(denominator) + peak - chosen
    loss_ref[...] = jnp.sum(jnp.where(eye, loss, 0.0), axis=0, keepdims=True)
    weights = (cycle_exp / denominator - jnp.where(positive, 1.0, 0.0)).astype(jnp.bfloat16)
    hard_weights = (hard_exp / denominator).astype(jnp.bfloat16)
    right_weights = dots(weights, order).astype(jnp.bfloat16)

    for start, w, rows_ref in ((0, weights, left_ref), (half, right_weights, right_ref)):
        all_weights = jnp.concatenate([w, hard_weights], axis=1)
        for chunk in range(0, half, 512):
            at = slice(start + chunk, start + chunk + 512)
            all_rows = [rows_ref[:, chunk : chunk + 512]] + [pool[:, at] for pool in (p0, p1, p2, p3)]
            grad = jnp.dot(all_weights, jnp.concatenate(all_rows, axis=0), preferred_element_type=jnp.float32)
            grad_ref[:, at] = grad.astype(jnp.bfloat16)


VMEM = functools.partial(pl.BlockSpec, memory_space=pltpu.VMEM)
SMEM = functools.partial(pl.BlockSpec, memory_space=pltpu.SMEM)


def small_call(kernel, outs, args, name, scalars=0, flops=2**33):
    return pl.pallas_call(
        kernel,
        out_shape=outs,
        in_specs=[SMEM()] * scalars + [VMEM()] * (len(args) - scalars),
        out_specs=jax.tree.map(lambda _: VMEM(), outs),
        compiler_params=pltpu.CompilerParams(vmem_limit_bytes=8 * 2**20),
        cost_estimate=pl.CostEstimate(flops=flops, bytes_accessed=4 * 2**20, transcendentals=0),
        name=name,
    )(*args)


def hard_call(place, refs, count, lists, queries, pool):
    rows = queries.shape[0]
    out = jax.ShapeDtypeStruct((rows, 4 * lists.size), jnp.float32)
    args = (place, refs.T, count.reshape(1, rows), lists[0], queries, pool)
    return small_call(hard_kernel, out, args, "hard", scalars=1)


def hard_rest_call(hard, queries, pools):
    out = jax.ShapeDtypeStruct(hard.shape, hard.dtype)
    return small_call(hard_rest_kernel, out, (hard, queries, *pools), "hard_rest")


def sort_call(place, mine, theirs):
    out = jax.ShapeDtypeStruct((2, BLOCK, mine.shape[2]), mine.dtype)
    return small_call(sort_kernel, (out, out, out), (place, mine, theirs), "sort", scalars=1)


def hand_call(left, right):
    out = jax.ShapeDtypeStruct(left.shape, left.dtype)
    one = jax.ShapeDtypeStruct((1,) + left.shape[1:], left.dtype)
    return small_call(hand_kernel, (one, one, out), (left, right), "hand")


def tail_call(place, positive, hard, queries, blocks, pools):
    rows, width = queries.shape
    half = width // 2
    return pl.pallas_call(
        tail_kernel,
        out_shape=(
            jax.ShapeDtypeStruct((rows, width), jnp.bfloat16),
            jax.ShapeDtypeStruct((1, rows), jnp.float32),
        ),
        in_specs=[SMEM()] + [VMEM()] * (3 + len(blocks) + len(pools)),
        out_specs=(VMEM(), VMEM()),
        scratch_shapes=[pltpu.VMEM((8 * BLOCK, half), jnp.bfloat16), pltpu.VMEM((8 * BLOCK, half), jnp.bfloat16)],
        compiler_params=pltpu.CompilerParams(vmem_limit_bytes=16 * 2**20),
        cost_estimate=pl.CostEstimate(flops=2**31, bytes_accessed=12 * 2**20, transcendentals=2**17),
        name="tail",
    )(place, positive.reshape(1, rows), hard, queries, *blocks, *pools)


def body(queries, passages, pool, positive_ids, request_lists, hard_refs, hard_count):
    half = passages.shape[1] // 2
    device = lax.axis_index("d")
    core = device & 1
    place = jnp.stack([device >> 7, (device >> 2) & 7, core, device & 3]).astype(jnp.int32)

    with jax.named_scope("cross"):
        halves = passages.reshape(2, 2, half).transpose(1, 0, 2)
        sent = jnp.broadcast_to(halves[None], (4, 2, 2, half)).reshape(8, 2, half)
        got = lax.all_to_all(sent, "d", 0, 0, axis_index_groups=CROSS, tiled=True)
    with jax.named_scope("own_pool"):
        hard = hard_call(place, hard_refs, hard_count, request_lists, queries, pool)
    got, hard = lax.optimization_barrier((got, hard))
    with jax.named_scope("near"):
        got = got.reshape(4, 2, 2, half).transpose(1, 0, 2, 3).reshape(1, 16, half)
        sent = jnp.broadcast_to(got, (8, 16, half))
        near = lax.all_to_all(sent, "d", 0, 0, axis_index_groups=NEAR, tiled=True)
        theirs = lax.ppermute(near, "d", OTHER_CORE)
        left, right, keep = sort_call(place, near, theirs)
    with jax.named_scope("pool_x"):
        near, pool = lax.optimization_barrier((near, pool))
        pool_x = lax.ppermute(pool, "d", OTHER_CHIP)
    with jax.named_scope("ring"):
        blocks = [keep]
        for step in range(3):
            left, right = lax.ppermute(left, "d", RING_Z), lax.ppermute(right, "d", RING_Y)
            if step == 0:
                left, pool = lax.optimization_barrier((left, pool))
                pool_c = lax.ppermute(pool, "d", OTHER_CORE)
            if step == 2:
                left, right, *blocks = lax.optimization_barrier((left, right, *blocks))
            keep_left, keep_right, give = hand_call(left, right)
            blocks += [keep_left, keep_right, lax.ppermute(give, "d", OTHER_CORE)]
        blocks += [lax.ppermute(keep_left, "d", RING_Z), lax.ppermute(keep_right, "d", RING_Y)]
    with jax.named_scope("other_pools"):
        pool_xc = lax.ppermute(pool_x, "d", OTHER_CORE)
        pools = (pool, pool_c, pool_x, pool_xc)
        hard = hard_rest_call(hard, queries, pools[1:])
    grad, loss = tail_call(place, positive_ids, hard, queries, blocks, pools)
    return grad, loss.reshape(-1)


def solution(mesh):
    flat = Mesh(mesh.devices.reshape(1024), ("d",))
    return jax.shard_map(
        body,
        mesh=flat,
        in_specs=(P("d", None), P("d", None), P("d", None), P("d"), P("d", None, None), P("d", None), P("d")),
        out_specs=(P("d", None), P("d")),
        check_vma=False,
    )
```

```python
import functools

import jax
import jax.numpy as jnp
import numpy as np
from jax import lax
from jax.experimental import pallas as pl
from jax.experimental.pallas import tpu as pltpu
from jax.sharding import Mesh, PartitionSpec as P

DEVICES = np.arange(1024).reshape(8, 4, 8, 2, 2)


def lines(order):
    return DEVICES.transpose(order)


ALONG_Y = lines((0, 1, 3, 4, 2))
ALONG_Z = lines((1, 2, 3, 4, 0))
CROSS = lines((0, 2, 3, 1, 4)).reshape(-1, 8).tolist()
NEAR = np.concatenate([ALONG_Y[:, :, :, 0].reshape(-1, 8), ALONG_Z[:, :, :, 1].reshape(-1, 8)]).tolist()


def ring(groups):
    return [(g[i], g[(i + 1 - 2 * (g[i] & 1)) % 8]) for g in groups.reshape(-1, 8) for i in range(8)]


RING_Z = ring(ALONG_Z)
RING_Y = ring(ALONG_Y)
OTHER_CORE = [(i, i ^ 1) for i in range(1024)]
OTHER_CHIP = [(i, i ^ 2) for i in range(1024)]
BLOCK = 64


def dots(a, b):
    return lax.dot_general(a, b, (((1,), (1,)), ((), ())), preferred_element_type=jnp.float32)


def mask_kernel(place_ref, refs_ref, count_ref, list_ref, out_ref):
    most, rows = refs_ref.shape
    owners, slots = list_ref.shape
    span = owners * slots
    own = place_ref[3]
    at = lax.broadcasted_iota(jnp.int32, (span, rows), 0)
    live = lax.broadcasted_iota(jnp.int32, (most, rows), 0) < count_ref[...]
    refs = jnp.where(live, refs_ref[...], -1)
    present = jnp.zeros((span, rows), jnp.float32)
    for i in range(most):
        present = present + jnp.where(refs[i : i + 1, :] == at, 1.0, 0.0)
    present = present.astype(jnp.bfloat16)
    row = lax.broadcasted_iota(jnp.int32, (span, span), 0)
    owner = lax.broadcasted_iota(jnp.int32, (span, span), 1) // slots
    lists = jnp.concatenate([list_ref[i : i + 1, :] for i in range(owners)], axis=1)
    same = lists == row
    for i in range(4):
        match = jnp.where(same & (owner == (own ^ i)), 1.0, 0.0).astype(jnp.bfloat16)
        used = lax.dot_general(present, match, (((0,), (1,)), ((), ())), preferred_element_type=jnp.float32)
        out_ref[:, i * span : (i + 1) * span] = jnp.where(used > 0, 0.0, -jnp.inf)


def hard_kernel(mask_ref, q_ref, p0, p1, p2, p3, out_ref):
    span = p0.shape[0]
    for i, pool in enumerate((p0, p1, p2, p3)):
        at = slice(i * span, (i + 1) * span)
        out_ref[:, at] = mask_ref[:, at] + dots(q_ref[...], pool[...])


def copies_kernel(x_ref, out_ref):
    half = out_ref.shape[2]
    for i in range(out_ref.shape[0]):
        out_ref[i] = x_ref[:, (i % 2) * half : (i % 2 + 1) * half]


def passage(shape, dim, place, ring_is_z):
    at = lax.broadcasted_iota(jnp.int32, shape, dim)
    block, inner, hi, row = at >> 6, (at >> 3) & 7, (at >> 1) & 3, at & 1
    step = (block + 1) >> 1
    below = (block & 1) != place[2]
    shift = jnp.where(below, 8 - step, step)
    if ring_is_z:
        z, y = (place[0] + shift) & 7, inner
    else:
        z, y = inner, (place[1] + shift) & 7
    return ((z * 4 + hi) * 8 + y) * 2 + row


def sort_kernel(place_ref, mine_ref, theirs_ref, left_ref, right_ref, keep_ref):
    core = place_ref[2]
    own = 8 * core

    def order(source, target):
        for i in range(8):
            piece = source[i]
            first, second = piece[:8], piece[8:]
            at = slice(8 * i, 8 * i + 8)
            target[0, at] = jnp.where(own == 0, first, second)
            target[1, at] = jnp.where(own == 0, second, first)

    @pl.when(core == 0)
    def _():
        order(mine_ref, left_ref)
        order(theirs_ref, right_ref)

    @pl.when(core == 1)
    def _():
        order(theirs_ref, left_ref)
        order(mine_ref, right_ref)

    keep_ref[0] = left_ref[0]
    keep_ref[1] = right_ref[0]


def hand_kernel(left_ref, right_ref, keep_left_ref, keep_right_ref, give_ref):
    keep_left_ref[0] = left_ref[0]
    keep_right_ref[0] = right_ref[0]
    give_ref[0] = left_ref[1]
    give_ref[1] = right_ref[1]


def tail_kernel(place_ref, pos_ref, hard_ref, q_ref, *rest):
    blocks, (p0, p1, p2, p3), (grad_ref, loss_ref, left_ref, right_ref) = rest[:12], rest[12:16], rest[16:20]
    out_ref, sems = rest[20:]
    keep, l1, r1, e1, l2, r2, e2, l3, r3, e3, l4, r4 = blocks
    half = left_ref.shape[1]
    total = left_ref.shape[0]
    lefts = (keep.at[0], l1.at[0], e1.at[0], l2.at[0], e2.at[0], l3.at[0], e3.at[0], l4.at[0])
    rights = (keep.at[1], r1.at[0], e1.at[1], r2.at[0], e2.at[1], r3.at[0], e3.at[1], r4.at[0])
    for parts, rows_ref in ((lefts, left_ref), (rights, right_ref)):
        for i, part in enumerate(parts):
            rows_ref[i * BLOCK : (i + 1) * BLOCK, :] = part[...]

    place = (place_ref[0], place_ref[1], place_ref[2])
    left_index = passage((1, total), 1, place, True)
    right_index = passage((total, 1), 0, place, False)
    order = jnp.where(right_index == left_index, 1.0, 0.0).astype(jnp.bfloat16)
    right_logits = dots(q_ref[:, half:], right_ref[...])
    high = right_logits.astype(jnp.bfloat16)
    left_over = right_logits - high.astype(jnp.float32)
    middle = left_over.astype(jnp.bfloat16)
    low = (left_over - middle.astype(jnp.float32)).astype(jnp.bfloat16)
    moved = jnp.dot(low, order, preferred_element_type=jnp.float32)
    moved = moved + jnp.dot(middle, order, preferred_element_type=jnp.float32)
    moved = moved + jnp.dot(high, order, preferred_element_type=jnp.float32)
    logits = dots(q_ref[:, :half], left_ref[...]) + moved

    hard = hard_ref[...]
    peak = jnp.maximum(jnp.max(logits, axis=1, keepdims=True), jnp.max(hard, axis=1, keepdims=True))
    cycle_exp = jnp.exp(logits - peak)
    hard_exp = jnp.exp(hard - peak)
    denominator = jnp.sum(cycle_exp, axis=1, keepdims=True) + jnp.sum(hard_exp, axis=1, keepdims=True)
    rows = q_ref.shape[0]
    eye = lax.broadcasted_iota(jnp.int32, (rows, rows), 0) == lax.broadcasted_iota(jnp.int32, (rows, rows), 1)
    positives = jnp.sum(jnp.where(eye, pos_ref[...].astype(jnp.float32), 0.0), axis=1, keepdims=True)
    positive = left_index == positives.astype(jnp.int32)
    chosen = jnp.sum(jnp.where(positive, logits, 0.0), axis=1, keepdims=True)
    loss = jnp.log(denominator) + peak - chosen
    loss_ref[...] = jnp.sum(jnp.where(eye, loss, 0.0), axis=0, keepdims=True)
    weights = (cycle_exp / denominator - jnp.where(positive, 1.0, 0.0)).astype(jnp.bfloat16)
    hard_weights = (hard_exp / denominator).astype(jnp.bfloat16)
    right_weights = dots(weights, order).astype(jnp.bfloat16)

    copies = []
    for start, w, rows_ref in ((0, weights, left_ref), (half, right_weights, right_ref)):
        all_weights = jnp.concatenate([w, hard_weights], axis=1)
        for chunk in range(0, half, 512):
            at = slice(start + chunk, start + chunk + 512)
            all_rows = [rows_ref[:, chunk : chunk + 512]] + [pool[:, at] for pool in (p0, p1, p2, p3)]
            grad = jnp.dot(all_weights, jnp.concatenate(all_rows, axis=0), preferred_element_type=jnp.float32)
            out_ref[:, at] = grad.astype(jnp.bfloat16)
            copy = pltpu.make_async_copy(out_ref.at[:, at], grad_ref.at[:, at], sems.at[len(copies)])
            copy.start()
            copies.append(copy)
    for copy in copies:
        copy.wait()


VMEM = functools.partial(pl.BlockSpec, memory_space=pltpu.VMEM)
SMEM = functools.partial(pl.BlockSpec, memory_space=pltpu.SMEM)


def small_call(kernel, outs, args, name, scalars=0, flops=2**33):
    return pl.pallas_call(
        kernel,
        out_shape=outs,
        in_specs=[SMEM()] * scalars + [VMEM()] * (len(args) - scalars),
        out_specs=jax.tree.map(lambda _: VMEM(), outs),
        compiler_params=pltpu.CompilerParams(vmem_limit_bytes=8 * 2**20),
        cost_estimate=pl.CostEstimate(flops=flops, bytes_accessed=4 * 2**20, transcendentals=0),
        name=name,
    )(*args)


def mask_call(place, refs, count, lists):
    rows = refs.shape[0]
    out = jax.ShapeDtypeStruct((rows, 4 * lists.size), jnp.float32)
    return small_call(mask_kernel, out, (place, refs.T, count.reshape(1, rows), lists[0]), "mask", scalars=1)


def hard_call(mask, queries, pools):
    out = jax.ShapeDtypeStruct(mask.shape, mask.dtype)
    return small_call(hard_kernel, out, (mask, queries, *pools), "hard")


def copies_call(passages):
    rows, width = passages.shape
    out = jax.ShapeDtypeStruct((8, rows, width // 2), passages.dtype)
    return small_call(copies_kernel, out, (passages,), "copies", flops=2**20)


def sort_call(place, mine, theirs):
    out = jax.ShapeDtypeStruct((2, BLOCK, mine.shape[2]), mine.dtype)
    return small_call(sort_kernel, (out, out, out), (place, mine, theirs), "sort", scalars=1)


def hand_call(left, right):
    out = jax.ShapeDtypeStruct(left.shape, left.dtype)
    one = jax.ShapeDtypeStruct((1,) + left.shape[1:], left.dtype)
    return small_call(hand_kernel, (one, one, out), (left, right), "hand")


def tail_call(place, positive, hard, queries, blocks, pools):
    rows, width = queries.shape
    half = width // 2
    return pl.pallas_call(
        tail_kernel,
        out_shape=(
            jax.ShapeDtypeStruct((rows, width), jnp.bfloat16),
            jax.ShapeDtypeStruct((1, rows), jnp.float32),
        ),
        in_specs=[SMEM()] + [VMEM()] * (3 + len(blocks) + len(pools)),
        out_specs=(pl.BlockSpec(memory_space=pl.ANY), VMEM()),
        scratch_shapes=[
            pltpu.VMEM((8 * BLOCK, half), jnp.bfloat16),
            pltpu.VMEM((8 * BLOCK, half), jnp.bfloat16),
            pltpu.VMEM((rows, width), jnp.bfloat16),
            pltpu.SemaphoreType.DMA((8,)),
        ],
        compiler_params=pltpu.CompilerParams(vmem_limit_bytes=16 * 2**20),
        cost_estimate=pl.CostEstimate(flops=2**31, bytes_accessed=12 * 2**20, transcendentals=2**17),
        name="tail",
    )(place, positive.reshape(1, rows), hard, queries, *blocks, *pools)


def body(queries, passages, pool, positive_ids, request_lists, hard_refs, hard_count):
    half = passages.shape[1] // 2
    device = lax.axis_index("d")
    core = device & 1
    place = jnp.stack([device >> 7, (device >> 2) & 7, core, device & 3]).astype(jnp.int32)

    with jax.named_scope("cross"):
        got = lax.all_to_all(copies_call(passages), "d", 0, 0, axis_index_groups=CROSS, tiled=True)
    with jax.named_scope("used"):
        mask = mask_call(place, hard_refs, hard_count, request_lists)
    got, mask = lax.optimization_barrier((got, mask))
    with jax.named_scope("near"):
        got = got.reshape(4, 2, 2, half).transpose(1, 0, 2, 3).reshape(1, 16, half)
        sent = jnp.broadcast_to(got, (8, 16, half))
        near = lax.all_to_all(sent, "d", 0, 0, axis_index_groups=NEAR, tiled=True)
        theirs = lax.ppermute(near, "d", OTHER_CORE)
        left, right, keep = sort_call(place, near, theirs)
    with jax.named_scope("pool_x"):
        near, pool = lax.optimization_barrier((near, pool))
        pool_x = lax.ppermute(pool, "d", OTHER_CHIP)
    with jax.named_scope("ring"):
        blocks = [keep]
        left, right = lax.ppermute(left, "d", RING_Z), lax.ppermute(right, "d", RING_Y)
        for step in range(3):
            if step == 0:
                left, pool = lax.optimization_barrier((left, pool))
            if step == 1:
                _, pool_x = lax.optimization_barrier((left, pool_x))
            if step == 2:
                left, right, *blocks = lax.optimization_barrier((left, right, *blocks))
            else:
                next_left, next_right = lax.ppermute(left, "d", RING_Z), lax.ppermute(right, "d", RING_Y)
            keep_left, keep_right, give = hand_call(left, right)
            if step == 2:
                next_left, next_right = lax.ppermute(keep_left, "d", RING_Z), lax.ppermute(keep_right, "d", RING_Y)
            blocks += [keep_left, keep_right, lax.ppermute(give, "d", OTHER_CORE)]
            left, right = next_left, next_right
        blocks += [left, right]
    with jax.named_scope("other_pools"):
        pool_c, pool_xc = lax.ppermute(pool, "d", OTHER_CORE), lax.ppermute(pool_x, "d", OTHER_CORE)
        pools = (pool, pool_c, pool_x, pool_xc)
        hard = hard_call(mask, queries, pools)
    grad, loss = tail_call(place, positive_ids, hard, queries, blocks, pools)
    return grad, loss.reshape(-1)


def solution(mesh):
    flat = Mesh(mesh.devices.reshape(1024), ("d",))
    return jax.shard_map(
        body,
        mesh=flat,
        in_specs=(P("d", None), P("d", None), P("d", None), P("d"), P("d", None, None), P("d", None), P("d")),
        out_specs=(P("d", None), P("d")),
        check_vma=False,
    )
```

```python
import functools

import jax
import jax.numpy as jnp
import numpy as np
from jax import lax
from jax.experimental import pallas as pl
from jax.experimental.pallas import tpu as pltpu
from jax.sharding import Mesh, PartitionSpec as P

DEVICES = np.arange(1024).reshape(8, 4, 8, 2, 2)


def lines(order):
    return DEVICES.transpose(order)


ALONG_Y = lines((0, 1, 3, 4, 2))
ALONG_Z = lines((1, 2, 3, 4, 0))
CROSS = lines((0, 2, 3, 1, 4)).reshape(-1, 8).tolist()
NEAR = np.concatenate([ALONG_Y[:, :, :, 0].reshape(-1, 8), ALONG_Z[:, :, :, 1].reshape(-1, 8)]).tolist()


def ring(groups, far=1):
    return [(g[i], g[(i + far * (1 - 2 * (g[i] & 1))) % 8]) for g in groups.reshape(-1, 8) for i in range(8)]


RING_Z = ring(ALONG_Z)
RING_Y = ring(ALONG_Y)
RING_Z2 = ring(ALONG_Z, 2)
RING_Y2 = ring(ALONG_Y, 2)
OTHER_CORE = [(i, i ^ 1) for i in range(1024)]
OTHER_CHIP = [(i, i ^ 2) for i in range(1024)]
BLOCK = 64


def dots(a, b):
    return lax.dot_general(a, b, (((1,), (1,)), ((), ())), preferred_element_type=jnp.float32)


def mask_kernel(place_ref, refs_ref, count_ref, list_ref, out_ref):
    most, rows = refs_ref.shape
    owners, slots = list_ref.shape
    span = owners * slots
    own = place_ref[3]
    at = lax.broadcasted_iota(jnp.int32, (span, rows), 0)
    live = lax.broadcasted_iota(jnp.int32, (most, rows), 0) < count_ref[...]
    refs = jnp.where(live, refs_ref[...], -1)
    present = jnp.zeros((span, rows), jnp.float32)
    for i in range(most):
        present = present + jnp.where(refs[i : i + 1, :] == at, 1.0, 0.0)
    present = present.astype(jnp.bfloat16)
    row = lax.broadcasted_iota(jnp.int32, (span, span), 0)
    owner = lax.broadcasted_iota(jnp.int32, (span, span), 1) // slots
    lists = jnp.concatenate([list_ref[i : i + 1, :] for i in range(owners)], axis=1)
    same = lists == row
    for i in range(4):
        match = jnp.where(same & (owner == (own ^ i)), 1.0, 0.0).astype(jnp.bfloat16)
        used = lax.dot_general(present, match, (((0,), (1,)), ((), ())), preferred_element_type=jnp.float32)
        out_ref[:, i * span : (i + 1) * span] = jnp.where(used > 0, 0.0, -jnp.inf)


def hard_kernel(mask_ref, q_ref, p0, p1, p2, p3, out_ref):
    span = p0.shape[0]
    for i, pool in enumerate((p0, p1, p2, p3)):
        at = slice(i * span, (i + 1) * span)
        out_ref[:, at] = mask_ref[:, at] + dots(q_ref[...], pool[...])


def copies_kernel(x_ref, out_ref):
    half = out_ref.shape[2]
    for i in range(out_ref.shape[0]):
        out_ref[i] = x_ref[:, (i % 2) * half : (i % 2 + 1) * half]


def passage(shape, dim, place, ring_is_z):
    at = lax.broadcasted_iota(jnp.int32, shape, dim)
    block, inner, hi, row = at >> 6, (at >> 3) & 7, (at >> 1) & 3, at & 1
    step = (block + 1) >> 1
    below = (block & 1) != place[2]
    shift = jnp.where(below, 8 - step, step)
    if ring_is_z:
        z, y = (place[0] + shift) & 7, inner
    else:
        z, y = inner, (place[1] + shift) & 7
    return ((z * 4 + hi) * 8 + y) * 2 + row


def sort_kernel(place_ref, mine_ref, theirs_ref, left_ref, right_ref, keep_ref):
    core = place_ref[2]
    own = 8 * core

    def order(source, target):
        for i in range(8):
            piece = source[i]
            first, second = piece[:8], piece[8:]
            at = slice(8 * i, 8 * i + 8)
            target[0, at] = jnp.where(own == 0, first, second)
            target[1, at] = jnp.where(own == 0, second, first)

    @pl.when(core == 0)
    def _():
        order(mine_ref, left_ref)
        order(theirs_ref, right_ref)

    @pl.when(core == 1)
    def _():
        order(theirs_ref, left_ref)
        order(mine_ref, right_ref)

    keep_ref[0] = left_ref[0]
    keep_ref[1] = right_ref[0]


def hand_kernel(left_ref, right_ref, *rest):
    waiting, (keep_left_ref, keep_right_ref, give_ref) = rest[:-3], rest[-3:]
    keep_left_ref[0] = left_ref[0]
    keep_right_ref[0] = right_ref[0]
    at = 0
    for part in waiting:
        give_ref[: part.shape[0]] = part[...]
        at = part.shape[0]
    give_ref[at] = left_ref[1]
    give_ref[at + 1] = right_ref[1]


def tail_kernel(place_ref, pos_ref, hard_ref, q_ref, *rest):
    blocks, (p0, p1, p2, p3), (grad_ref, loss_ref, left_ref, right_ref) = rest[:11], rest[11:15], rest[15:19]
    out_ref, sems = rest[19:]
    keep, l1, r1, e1, l2, r2, l3, r3, e23, l4, r4 = blocks
    half = left_ref.shape[1]
    total = left_ref.shape[0]
    lefts = (keep.at[0], l1.at[0], e1.at[0], l2.at[0], e23.at[0], l3.at[0], e23.at[2], l4.at[0])
    rights = (keep.at[1], r1.at[0], e1.at[1], r2.at[0], e23.at[1], r3.at[0], e23.at[3], r4.at[0])
    for parts, rows_ref in ((lefts, left_ref), (rights, right_ref)):
        for i, part in enumerate(parts):
            rows_ref[i * BLOCK : (i + 1) * BLOCK, :] = part[...]

    place = (place_ref[0], place_ref[1], place_ref[2])
    left_index = passage((1, total), 1, place, True)
    right_index = passage((total, 1), 0, place, False)
    order = jnp.where(right_index == left_index, 1.0, 0.0).astype(jnp.bfloat16)
    right_logits = dots(q_ref[:, half:], right_ref[...])
    high = right_logits.astype(jnp.bfloat16)
    left_over = right_logits - high.astype(jnp.float32)
    middle = left_over.astype(jnp.bfloat16)
    low = (left_over - middle.astype(jnp.float32)).astype(jnp.bfloat16)
    moved = jnp.dot(low, order, preferred_element_type=jnp.float32)
    moved = moved + jnp.dot(middle, order, preferred_element_type=jnp.float32)
    moved = moved + jnp.dot(high, order, preferred_element_type=jnp.float32)
    logits = dots(q_ref[:, :half], left_ref[...]) + moved

    hard = hard_ref[...]
    peak = jnp.maximum(jnp.max(logits, axis=1, keepdims=True), jnp.max(hard, axis=1, keepdims=True))
    cycle_exp = jnp.exp(logits - peak)
    hard_exp = jnp.exp(hard - peak)
    denominator = jnp.sum(cycle_exp, axis=1, keepdims=True) + jnp.sum(hard_exp, axis=1, keepdims=True)
    rows = q_ref.shape[0]
    eye = lax.broadcasted_iota(jnp.int32, (rows, rows), 0) == lax.broadcasted_iota(jnp.int32, (rows, rows), 1)
    positives = jnp.sum(jnp.where(eye, pos_ref[...].astype(jnp.float32), 0.0), axis=1, keepdims=True)
    positive = left_index == positives.astype(jnp.int32)
    chosen = jnp.sum(jnp.where(positive, logits, 0.0), axis=1, keepdims=True)
    loss = jnp.log(denominator) + peak - chosen
    loss_ref[...] = jnp.sum(jnp.where(eye, loss, 0.0), axis=0, keepdims=True)
    weights = (cycle_exp / denominator - jnp.where(positive, 1.0, 0.0)).astype(jnp.bfloat16)
    hard_weights = (hard_exp / denominator).astype(jnp.bfloat16)
    right_weights = dots(weights, order).astype(jnp.bfloat16)

    copies = []
    for start, w, rows_ref in ((0, weights, left_ref), (half, right_weights, right_ref)):
        all_weights = jnp.concatenate([w, hard_weights], axis=1)
        for chunk in range(0, half, 512):
            at = slice(start + chunk, start + chunk + 512)
            all_rows = [rows_ref[:, chunk : chunk + 512]] + [pool[:, at] for pool in (p0, p1, p2, p3)]
            grad = jnp.dot(all_weights, jnp.concatenate(all_rows, axis=0), preferred_element_type=jnp.float32)
            out_ref[:, at] = grad.astype(jnp.bfloat16)
            copy = pltpu.make_async_copy(out_ref.at[:, at], grad_ref.at[:, at], sems.at[len(copies)])
            copy.start()
            copies.append(copy)
    for copy in copies:
        copy.wait()


VMEM = functools.partial(pl.BlockSpec, memory_space=pltpu.VMEM)
SMEM = functools.partial(pl.BlockSpec, memory_space=pltpu.SMEM)


def small_call(kernel, outs, args, name, scalars=0, flops=2**33):
    return pl.pallas_call(
        kernel,
        out_shape=outs,
        in_specs=[SMEM()] * scalars + [VMEM()] * (len(args) - scalars),
        out_specs=jax.tree.map(lambda _: VMEM(), outs),
        compiler_params=pltpu.CompilerParams(vmem_limit_bytes=8 * 2**20),
        cost_estimate=pl.CostEstimate(flops=flops, bytes_accessed=4 * 2**20, transcendentals=0),
        name=name,
    )(*args)


def mask_call(place, refs, count, lists):
    rows = refs.shape[0]
    out = jax.ShapeDtypeStruct((rows, 4 * lists.size), jnp.float32)
    return small_call(mask_kernel, out, (place, refs.T, count.reshape(1, rows), lists[0]), "mask", scalars=1)


def hard_call(mask, queries, pools):
    out = jax.ShapeDtypeStruct(mask.shape, mask.dtype)
    return small_call(hard_kernel, out, (mask, queries, *pools), "hard", flops=2**34)


def copies_call(passages):
    rows, width = passages.shape
    out = jax.ShapeDtypeStruct((8, rows, width // 2), passages.dtype)
    return small_call(copies_kernel, out, (passages,), "copies", flops=2**20)


def sort_call(place, mine, theirs):
    out = jax.ShapeDtypeStruct((2, BLOCK, mine.shape[2]), mine.dtype)
    return small_call(sort_kernel, (out, out, out), (place, mine, theirs), "sort", scalars=1)


def hand_call(left, right, *waiting, flops=2**33):
    one = jax.ShapeDtypeStruct((1,) + left.shape[1:], left.dtype)
    out = jax.ShapeDtypeStruct((2 + sum(part.shape[0] for part in waiting),) + left.shape[1:], left.dtype)
    return small_call(hand_kernel, (one, one, out), (left, right, *waiting), "hand", flops=flops)


def tail_call(place, positive, hard, queries, blocks, pools):
    rows, width = queries.shape
    half = width // 2
    return pl.pallas_call(
        tail_kernel,
        out_shape=(
            jax.ShapeDtypeStruct((rows, width), jnp.bfloat16),
            jax.ShapeDtypeStruct((1, rows), jnp.float32),
        ),
        in_specs=[SMEM()] + [VMEM()] * (3 + len(blocks) + len(pools)),
        out_specs=(pl.BlockSpec(memory_space=pl.ANY), VMEM()),
        scratch_shapes=[
            pltpu.VMEM((8 * BLOCK, half), jnp.bfloat16),
            pltpu.VMEM((8 * BLOCK, half), jnp.bfloat16),
            pltpu.VMEM((rows, width), jnp.bfloat16),
            pltpu.SemaphoreType.DMA((8,)),
        ],
        compiler_params=pltpu.CompilerParams(vmem_limit_bytes=16 * 2**20),
        cost_estimate=pl.CostEstimate(flops=2**31, bytes_accessed=12 * 2**20, transcendentals=2**17),
        name="tail",
    )(place, positive.reshape(1, rows), hard, queries, *blocks, *pools)


def body(queries, passages, pool, positive_ids, request_lists, hard_refs, hard_count):
    half = passages.shape[1] // 2
    device = lax.axis_index("d")
    core = device & 1
    place = jnp.stack([device >> 7, (device >> 2) & 7, core, device & 3]).astype(jnp.int32)

    with jax.named_scope("cross"):
        got = lax.all_to_all(copies_call(passages), "d", 0, 0, axis_index_groups=CROSS, tiled=True)
    with jax.named_scope("used"):
        mask = mask_call(place, hard_refs, hard_count, request_lists)
    got, mask = lax.optimization_barrier((got, mask))
    with jax.named_scope("near"):
        got = got.reshape(4, 2, 2, half).transpose(1, 0, 2, 3).reshape(1, 16, half)
        sent = jnp.broadcast_to(got, (8, 16, half))
        near = lax.all_to_all(sent, "d", 0, 0, axis_index_groups=NEAR, tiled=True)
        theirs = lax.ppermute(near, "d", OTHER_CORE)
        left, right, keep = sort_call(place, near, theirs)
    with jax.named_scope("pool_x"):
        near, pool = lax.optimization_barrier((near, pool))
        pool_x = lax.ppermute(pool, "d", OTHER_CHIP)
    with jax.named_scope("ring"):
        blocks = [keep]
        left, right = lax.ppermute(left, "d", RING_Z), lax.ppermute(right, "d", RING_Y)
        pool_c = lax.ppermute(pool, "d", OTHER_CORE)
        for step in range(3):
            waiting = ()
            if step < 2:
                next_left, next_right = lax.ppermute(left, "d", RING_Z), lax.ppermute(right, "d", RING_Y)
            else:
                left, right, *blocks = lax.optimization_barrier((left, right, *blocks))
                waiting = (give,)
            if step == 0:
                left, pool_c = lax.optimization_barrier((left, pool_c))
            keep_left, keep_right, give = hand_call(left, right, *waiting, flops=2**33 if step < 2 else 2**35)
            blocks += [keep_left, keep_right]
            if step == 1:
                _, pool_x = lax.optimization_barrier((give, pool_x))
                last = [lax.ppermute(keep_left, "d", RING_Z2), lax.ppermute(keep_right, "d", RING_Y2)]
            else:
                blocks.append(lax.ppermute(give, "d", OTHER_CORE))
            left, right = next_left, next_right
    with jax.named_scope("other_pools"):
        pool_xc = lax.ppermute(pool_x, "d", OTHER_CORE)
        pools = (pool, pool_c, pool_x, pool_xc)
        hard = hard_call(mask, queries, pools)
    grad, loss = tail_call(place, positive_ids, hard, queries, blocks + last, pools)
    return grad, loss.reshape(-1)


def solution(mesh):
    flat = Mesh(mesh.devices.reshape(1024), ("d",))
    return jax.shard_map(
        body,
        mesh=flat,
        in_specs=(P("d", None), P("d", None), P("d", None), P("d"), P("d", None, None), P("d", None), P("d")),
        out_specs=(P("d", None), P("d")),
        check_vma=False,
    )
```

```python
import functools

import jax
import jax.numpy as jnp
import numpy as np
from jax import lax
from jax.experimental import pallas as pl
from jax.experimental.pallas import tpu as pltpu
from jax.sharding import Mesh, PartitionSpec as P

DEVICES = np.arange(1024).reshape(8, 4, 8, 2, 2)


def lines(order):
    return DEVICES.transpose(order)


ALONG_Y = lines((0, 1, 3, 4, 2))
ALONG_Z = lines((1, 2, 3, 4, 0))
CROSS = lines((0, 2, 3, 1, 4)).reshape(-1, 8).tolist()
NEAR = np.concatenate([ALONG_Y[:, :, :, 0].reshape(-1, 8), ALONG_Z[:, :, :, 1].reshape(-1, 8)]).tolist()


def ring(groups, far=1):
    return [(g[i], g[(i + far * (1 - 2 * (g[i] & 1))) % 8]) for g in groups.reshape(-1, 8) for i in range(8)]


RING_Z = ring(ALONG_Z)
RING_Y = ring(ALONG_Y)
RING_Z2 = ring(ALONG_Z, 2)
RING_Y2 = ring(ALONG_Y, 2)
OTHER_CORE = [(i, i ^ 1) for i in range(1024)]
OTHER_CHIP = [(i, i ^ 2) for i in range(1024)]
BLOCK = 64


def dots(a, b):
    return lax.dot_general(a, b, (((1,), (1,)), ((), ())), preferred_element_type=jnp.float32)


def mask_kernel(place_ref, refs_ref, count_ref, list_ref, out_ref):
    most, rows = refs_ref.shape
    owners, slots = list_ref.shape
    span = owners * slots
    own = place_ref[3]
    at = lax.broadcasted_iota(jnp.int32, (span, rows), 0)
    live = lax.broadcasted_iota(jnp.int32, (most, rows), 0) < count_ref[...]
    refs = jnp.where(live, refs_ref[...], -1)
    present = jnp.zeros((span, rows), jnp.float32)
    for i in range(most):
        present = present + jnp.where(refs[i : i + 1, :] == at, 1.0, 0.0)
    present = present.astype(jnp.bfloat16)
    row = lax.broadcasted_iota(jnp.int32, (span, span), 0)
    owner = lax.broadcasted_iota(jnp.int32, (span, span), 1) // slots
    lists = jnp.concatenate([list_ref[i : i + 1, :] for i in range(owners)], axis=1)
    same = lists == row
    for i in range(4):
        match = jnp.where(same & (owner == (own ^ i)), 1.0, 0.0).astype(jnp.bfloat16)
        used = lax.dot_general(present, match, (((0,), (1,)), ((), ())), preferred_element_type=jnp.float32)
        out_ref[:, i * span : (i + 1) * span] = jnp.where(used > 0, 0.0, -jnp.inf)


def hard_kernel(mask_ref, q_ref, p0, p1, p2, p3, out_ref):
    span = p0.shape[0]
    for i, pool in enumerate((p0, p1, p2, p3)):
        at = slice(i * span, (i + 1) * span)
        out_ref[:, at] = mask_ref[:, at] + dots(q_ref[...], pool[...])


def copies_kernel(x_ref, out_ref):
    half = out_ref.shape[2]
    for i in range(out_ref.shape[0]):
        out_ref[i] = x_ref[:, (i % 2) * half : (i % 2 + 1) * half]


def passage(shape, dim, place, ring_is_z):
    at = lax.broadcasted_iota(jnp.int32, shape, dim)
    block, inner, hi, row = at >> 6, (at >> 3) & 7, (at >> 1) & 3, at & 1
    step = (block + 1) >> 1
    below = (block & 1) != place[2]
    shift = jnp.where(below, 8 - step, step)
    if ring_is_z:
        z, y = (place[0] + shift) & 7, inner
    else:
        z, y = inner, (place[1] + shift) & 7
    return ((z * 4 + hi) * 8 + y) * 2 + row


def sort_kernel(place_ref, mine_ref, theirs_ref, left_ref, right_ref, keep_ref):
    core = place_ref[2]
    own = 8 * core

    def order(source, target):
        for i in range(8):
            piece = source[i]
            first, second = piece[:8], piece[8:]
            at = slice(8 * i, 8 * i + 8)
            target[0, at] = jnp.where(own == 0, first, second)
            target[1, at] = jnp.where(own == 0, second, first)

    @pl.when(core == 0)
    def _():
        order(mine_ref, left_ref)
        order(theirs_ref, right_ref)

    @pl.when(core == 1)
    def _():
        order(theirs_ref, left_ref)
        order(mine_ref, right_ref)

    keep_ref[0] = left_ref[0]
    keep_ref[1] = right_ref[0]


def hand_kernel(left_ref, right_ref, *rest):
    waiting, (keep_left_ref, keep_right_ref, give_ref) = rest[:-3], rest[-3:]
    keep_left_ref[0] = left_ref[0]
    keep_right_ref[0] = right_ref[0]
    at = 0
    for part in waiting:
        give_ref[: part.shape[0]] = part[...]
        at = part.shape[0]
    give_ref[at] = left_ref[1]
    give_ref[at + 1] = right_ref[1]


def tail_kernel(place_ref, pos_ref, hard_ref, q_ref, *rest):
    blocks, (p0, p1, p2, p3), (grad_ref, loss_ref, left_ref, right_ref) = rest[:11], rest[11:15], rest[15:19]
    out_ref, sems = rest[19:]
    keep, l1, r1, e1, l2, r2, l3, r3, e23, l4, r4 = blocks
    half = left_ref.shape[1]
    total = left_ref.shape[0]
    lefts = (keep.at[0], l1.at[0], e1.at[0], l2.at[0], e23.at[0], l3.at[0], e23.at[2], l4.at[0])
    rights = (keep.at[1], r1.at[0], e1.at[1], r2.at[0], e23.at[1], r3.at[0], e23.at[3], r4.at[0])
    for parts, rows_ref in ((lefts, left_ref), (rights, right_ref)):
        for i, part in enumerate(parts):
            rows_ref[i * BLOCK : (i + 1) * BLOCK, :] = part[...]

    place = (place_ref[0], place_ref[1], place_ref[2])
    left_index = passage((1, total), 1, place, True)
    right_index = passage((total, 1), 0, place, False)
    order = jnp.where(right_index == left_index, 1.0, 0.0).astype(jnp.bfloat16)
    right_logits = dots(q_ref[:, half:], right_ref[...])
    high = right_logits.astype(jnp.bfloat16)
    left_over = right_logits - high.astype(jnp.float32)
    middle = left_over.astype(jnp.bfloat16)
    low = (left_over - middle.astype(jnp.float32)).astype(jnp.bfloat16)
    moved = jnp.dot(low, order, preferred_element_type=jnp.float32)
    moved = moved + jnp.dot(middle, order, preferred_element_type=jnp.float32)
    moved = moved + jnp.dot(high, order, preferred_element_type=jnp.float32)
    logits = dots(q_ref[:, :half], left_ref[...]) + moved

    hard = hard_ref[...]
    peak = jnp.maximum(jnp.max(logits, axis=1, keepdims=True), jnp.max(hard, axis=1, keepdims=True))
    cycle_exp = jnp.exp(logits - peak)
    hard_exp = jnp.exp(hard - peak)
    denominator = jnp.sum(cycle_exp, axis=1, keepdims=True) + jnp.sum(hard_exp, axis=1, keepdims=True)
    rows = q_ref.shape[0]
    eye = lax.broadcasted_iota(jnp.int32, (rows, rows), 0) == lax.broadcasted_iota(jnp.int32, (rows, rows), 1)
    positives = jnp.sum(jnp.where(eye, pos_ref[...].astype(jnp.float32), 0.0), axis=1, keepdims=True)
    positive = left_index == positives.astype(jnp.int32)
    chosen = jnp.sum(jnp.where(positive, logits, 0.0), axis=1, keepdims=True)
    loss = jnp.log(denominator) + peak - chosen
    loss_ref[...] = jnp.sum(jnp.where(eye, loss, 0.0), axis=0, keepdims=True)
    weights = (cycle_exp / denominator - jnp.where(positive, 1.0, 0.0)).astype(jnp.bfloat16)
    hard_weights = (hard_exp / denominator).astype(jnp.bfloat16)
    right_weights = dots(weights, order).astype(jnp.bfloat16)

    copies = []
    for start, w, rows_ref in ((0, weights, left_ref), (half, right_weights, right_ref)):
        all_weights = jnp.concatenate([w, hard_weights], axis=1)
        for chunk in range(0, half, 512):
            at = slice(start + chunk, start + chunk + 512)
            all_rows = [rows_ref[:, chunk : chunk + 512]] + [pool[:, at] for pool in (p0, p1, p2, p3)]
            grad = jnp.dot(all_weights, jnp.concatenate(all_rows, axis=0), preferred_element_type=jnp.float32)
            out_ref[:, at] = grad.astype(jnp.bfloat16)
            copy = pltpu.make_async_copy(out_ref.at[:, at], grad_ref.at[:, at], sems.at[len(copies)])
            copy.start()
            copies.append(copy)
    for copy in copies:
        copy.wait()


VMEM = functools.partial(pl.BlockSpec, memory_space=pltpu.VMEM)
SMEM = functools.partial(pl.BlockSpec, memory_space=pltpu.SMEM)


def small_call(kernel, outs, args, name, scalars=0, flops=2**33):
    return pl.pallas_call(
        kernel,
        out_shape=outs,
        in_specs=[SMEM()] * scalars + [VMEM()] * (len(args) - scalars),
        out_specs=jax.tree.map(lambda _: VMEM(), outs),
        compiler_params=pltpu.CompilerParams(vmem_limit_bytes=8 * 2**20),
        cost_estimate=pl.CostEstimate(flops=flops, bytes_accessed=4 * 2**20, transcendentals=0),
        name=name,
    )(*args)


def mask_call(place, refs, count, lists):
    rows = refs.shape[0]
    out = jax.ShapeDtypeStruct((rows, 4 * lists.size), jnp.float32)
    return small_call(mask_kernel, out, (place, refs.T, count.reshape(1, rows), lists[0]), "mask", scalars=1)


def hard_call(mask, queries, pools):
    out = jax.ShapeDtypeStruct(mask.shape, mask.dtype)
    return small_call(hard_kernel, out, (mask, queries, *pools), "hard", flops=2**34)


def copies_call(passages):
    rows, width = passages.shape
    out = jax.ShapeDtypeStruct((8, rows, width // 2), passages.dtype)
    return small_call(copies_kernel, out, (passages,), "copies", flops=2**20)


def sort_call(place, mine, theirs):
    out = jax.ShapeDtypeStruct((2, BLOCK, mine.shape[2]), mine.dtype)
    return small_call(sort_kernel, (out, out, out), (place, mine, theirs), "sort", scalars=1)


def hand_call(left, right, *waiting, flops=2**33):
    one = jax.ShapeDtypeStruct((1,) + left.shape[1:], left.dtype)
    out = jax.ShapeDtypeStruct((2 + sum(part.shape[0] for part in waiting),) + left.shape[1:], left.dtype)
    return small_call(hand_kernel, (one, one, out), (left, right, *waiting), "hand", flops=flops)


def tail_call(place, positive, hard, queries, blocks, pools):
    rows, width = queries.shape
    half = width // 2
    return pl.pallas_call(
        tail_kernel,
        out_shape=(
            jax.ShapeDtypeStruct((rows, width), jnp.bfloat16),
            jax.ShapeDtypeStruct((1, rows), jnp.float32),
        ),
        in_specs=[SMEM()] + [VMEM()] * (3 + len(blocks) + len(pools)),
        out_specs=(pl.BlockSpec(memory_space=pl.ANY), VMEM()),
        scratch_shapes=[
            pltpu.VMEM((8 * BLOCK, half), jnp.bfloat16),
            pltpu.VMEM((8 * BLOCK, half), jnp.bfloat16),
            pltpu.VMEM((rows, width), jnp.bfloat16),
            pltpu.SemaphoreType.DMA((8,)),
        ],
        compiler_params=pltpu.CompilerParams(vmem_limit_bytes=16 * 2**20),
        cost_estimate=pl.CostEstimate(flops=2**31, bytes_accessed=12 * 2**20, transcendentals=2**17),
        name="tail",
    )(place, positive.reshape(1, rows), hard, queries, *blocks, *pools)


def body(queries, passages, pool, positive_ids, request_lists, hard_refs, hard_count):
    half = passages.shape[1] // 2
    device = lax.axis_index("d")
    core = device & 1
    place = jnp.stack([device >> 7, (device >> 2) & 7, core, device & 3]).astype(jnp.int32)

    with jax.named_scope("cross"):
        got = lax.all_to_all(copies_call(passages), "d", 0, 0, axis_index_groups=CROSS, tiled=True)
    with jax.named_scope("used"):
        mask = mask_call(place, hard_refs, hard_count, request_lists)
    got, mask = lax.optimization_barrier((got, mask))
    with jax.named_scope("near"):
        got = got.reshape(4, 2, 2, half).transpose(1, 0, 2, 3).reshape(1, 16, half)
        sent = jnp.broadcast_to(got, (8, 16, half))
        near = lax.all_to_all(sent, "d", 0, 0, axis_index_groups=NEAR, tiled=True)
        theirs = lax.ppermute(near, "d", OTHER_CORE)
        left, right, keep = sort_call(place, near, theirs)
    with jax.named_scope("pool_x"):
        near, pool = lax.optimization_barrier((near, pool))
        pool_x = lax.ppermute(pool, "d", OTHER_CHIP)
    with jax.named_scope("ring"):
        blocks = [keep]
        left, right = lax.ppermute(left, "d", RING_Z), lax.ppermute(right, "d", RING_Y)
        pool_c = lax.ppermute(pool, "d", OTHER_CORE)
        for step in range(3):
            waiting = ()
            if step < 2:
                next_left, next_right = lax.ppermute(left, "d", RING_Z), lax.ppermute(right, "d", RING_Y)
            else:
                _, pool_x = lax.optimization_barrier((left, pool_x))
                left, right, *blocks = lax.optimization_barrier((left, right, *blocks))
                waiting = (give,)
            if step == 0:
                left, pool_c = lax.optimization_barrier((left, pool_c))
            keep_left, keep_right, give = hand_call(left, right, *waiting, flops=2**33 if step < 2 else 2**35)
            blocks += [keep_left, keep_right]
            if step == 1:
                last = [lax.ppermute(keep_left, "d", RING_Z2), lax.ppermute(keep_right, "d", RING_Y2)]
            else:
                blocks.append(lax.ppermute(give, "d", OTHER_CORE))
            left, right = next_left, next_right
    with jax.named_scope("other_pools"):
        pool_xc = lax.ppermute(pool_x, "d", OTHER_CORE)
        pools = (pool, pool_c, pool_x, pool_xc)
        hard = hard_call(mask, queries, pools)
    grad, loss = tail_call(place, positive_ids, hard, queries, blocks + last, pools)
    return grad, loss.reshape(-1)


def solution(mesh):
    flat = Mesh(mesh.devices.reshape(1024), ("d",))
    return jax.shard_map(
        body,
        mesh=flat,
        in_specs=(P("d", None), P("d", None), P("d", None), P("d"), P("d", None, None), P("d", None), P("d")),
        out_specs=(P("d", None), P("d")),
        check_vma=False,
    )
```

```python
import functools

import jax
import jax.numpy as jnp
import numpy as np
from jax import lax
from jax.experimental import pallas as pl
from jax.experimental.pallas import tpu as pltpu
from jax.sharding import Mesh, PartitionSpec as P

DEVICES = np.arange(1024).reshape(8, 4, 8, 2, 2)


def lines(order):
    return DEVICES.transpose(order)


ALONG_Y = lines((0, 1, 3, 4, 2))
ALONG_Z = lines((1, 2, 3, 4, 0))
CROSS = lines((0, 2, 3, 1, 4)).reshape(-1, 8).tolist()
NEAR = np.concatenate([ALONG_Y[:, :, :, 0].reshape(-1, 8), ALONG_Z[:, :, :, 1].reshape(-1, 8)]).tolist()


def ring(groups, far=1):
    return [(g[i], g[(i + far * (1 - 2 * (g[i] & 1))) % 8]) for g in groups.reshape(-1, 8) for i in range(8)]


RING_Z = ring(ALONG_Z)
RING_Y = ring(ALONG_Y)
RING_Z2 = ring(ALONG_Z, 2)
RING_Y2 = ring(ALONG_Y, 2)
OTHER_CORE = [(i, i ^ 1) for i in range(1024)]
OTHER_CHIP = [(i, i ^ 2) for i in range(1024)]
BLOCK = 64


def dots(a, b):
    return lax.dot_general(a, b, (((1,), (1,)), ((), ())), preferred_element_type=jnp.float32)


def mask_kernel(place_ref, refs_ref, count_ref, list_ref, out_ref):
    most, rows = refs_ref.shape
    owners, slots = list_ref.shape
    span = owners * slots
    own = place_ref[3]
    at = lax.broadcasted_iota(jnp.int32, (span, rows), 0)
    live = lax.broadcasted_iota(jnp.int32, (most, rows), 0) < count_ref[...]
    refs = jnp.where(live, refs_ref[...], -1)
    present = jnp.zeros((span, rows), jnp.float32)
    for i in range(most):
        present = present + jnp.where(refs[i : i + 1, :] == at, 1.0, 0.0)
    present = present.astype(jnp.bfloat16)
    row = lax.broadcasted_iota(jnp.int32, (span, span), 0)
    owner = lax.broadcasted_iota(jnp.int32, (span, span), 1) // slots
    lists = jnp.concatenate([list_ref[i : i + 1, :] for i in range(owners)], axis=1)
    same = lists == row
    for i in range(4):
        match = jnp.where(same & (owner == (own ^ i)), 1.0, 0.0).astype(jnp.bfloat16)
        used = lax.dot_general(present, match, (((0,), (1,)), ((), ())), preferred_element_type=jnp.float32)
        out_ref[:, i * span : (i + 1) * span] = jnp.where(used > 0, 0.0, -jnp.inf)


def hard_kernel(place_ref, pos_ref, mask_ref, q_ref, p0, p1, p2, p3, out_ref, order_ref, column_ref):
    total, rows = order_ref.shape[0], q_ref.shape[0]
    place = (place_ref[0], place_ref[1], place_ref[2])
    left_index = passage((1, total), 1, place, True)
    right_index = passage((total, 1), 0, place, False)
    order_ref[...] = jnp.where(right_index == left_index, 1.0, 0.0).astype(jnp.bfloat16)
    eye = lax.broadcasted_iota(jnp.int32, (rows, rows), 0) == lax.broadcasted_iota(jnp.int32, (rows, rows), 1)
    column_ref[...] = jnp.sum(jnp.where(eye, pos_ref[...].astype(jnp.float32), 0.0), axis=1, keepdims=True)
    span = p0.shape[0]
    for i, pool in enumerate((p0, p1, p2, p3)):
        at = slice(i * span, (i + 1) * span)
        out_ref[:, at] = mask_ref[:, at] + dots(q_ref[...], pool[...])


def copies_kernel(x_ref, out_ref):
    half = out_ref.shape[2]
    for i in range(out_ref.shape[0]):
        out_ref[i] = x_ref[:, (i % 2) * half : (i % 2 + 1) * half]


def passage(shape, dim, place, ring_is_z):
    at = lax.broadcasted_iota(jnp.int32, shape, dim)
    block, inner, hi, row = at >> 6, (at >> 3) & 7, (at >> 1) & 3, at & 1
    step = (block + 1) >> 1
    below = (block & 1) != place[2]
    shift = jnp.where(below, 8 - step, step)
    if ring_is_z:
        z, y = (place[0] + shift) & 7, inner
    else:
        z, y = inner, (place[1] + shift) & 7
    return ((z * 4 + hi) * 8 + y) * 2 + row


def sort_kernel(place_ref, mine_ref, theirs_ref, left_ref, right_ref, keep_ref):
    core = place_ref[2]
    own = 8 * core

    def order(source, target):
        for i in range(8):
            piece = source[i]
            first, second = piece[:8], piece[8:]
            at = slice(8 * i, 8 * i + 8)
            target[0, at] = jnp.where(own == 0, first, second)
            target[1, at] = jnp.where(own == 0, second, first)

    @pl.when(core == 0)
    def _():
        order(mine_ref, left_ref)
        order(theirs_ref, right_ref)

    @pl.when(core == 1)
    def _():
        order(theirs_ref, left_ref)
        order(mine_ref, right_ref)

    keep_ref[0] = left_ref[0]
    keep_ref[1] = right_ref[0]


def hand_kernel(left_ref, right_ref, *rest):
    waiting, (keep_left_ref, keep_right_ref, give_ref) = rest[:-3], rest[-3:]
    keep_left_ref[0] = left_ref[0]
    keep_right_ref[0] = right_ref[0]
    at = 0
    for part in waiting:
        give_ref[: part.shape[0]] = part[...]
        at = part.shape[0]
    give_ref[at] = left_ref[1]
    give_ref[at + 1] = right_ref[1]


def tail_kernel(place_ref, column_ref, hard_ref, order_ref, q_ref, *rest):
    blocks, (p0, p1, p2, p3), (grad_ref, loss_ref, left_ref, right_ref) = rest[:11], rest[11:15], rest[15:19]
    out_ref, sems = rest[19:]
    keep, l1, r1, e1, l2, r2, l3, r3, e23, l4, r4 = blocks
    half = left_ref.shape[1]
    total = left_ref.shape[0]
    lefts = (keep.at[0], l1.at[0], e1.at[0], l2.at[0], e23.at[0], l3.at[0], e23.at[2], l4.at[0])
    rights = (keep.at[1], r1.at[0], e1.at[1], r2.at[0], e23.at[1], r3.at[0], e23.at[3], r4.at[0])
    for parts, rows_ref in ((lefts, left_ref), (rights, right_ref)):
        for i, part in enumerate(parts):
            rows_ref[i * BLOCK : (i + 1) * BLOCK, :] = part[...]

    place = (place_ref[0], place_ref[1], place_ref[2])
    left_index = passage((1, total), 1, place, True)
    order = order_ref[...]
    right_logits = dots(q_ref[:, half:], right_ref[...])
    high = right_logits.astype(jnp.bfloat16)
    left_over = right_logits - high.astype(jnp.float32)
    middle = left_over.astype(jnp.bfloat16)
    low = (left_over - middle.astype(jnp.float32)).astype(jnp.bfloat16)
    moved = jnp.dot(low, order, preferred_element_type=jnp.float32)
    moved = moved + jnp.dot(middle, order, preferred_element_type=jnp.float32)
    moved = moved + jnp.dot(high, order, preferred_element_type=jnp.float32)
    logits = dots(q_ref[:, :half], left_ref[...]) + moved

    hard = hard_ref[...]
    peak = jnp.maximum(jnp.max(logits, axis=1, keepdims=True), jnp.max(hard, axis=1, keepdims=True))
    cycle_exp = jnp.exp(logits - peak)
    hard_exp = jnp.exp(hard - peak)
    denominator = jnp.sum(cycle_exp, axis=1, keepdims=True) + jnp.sum(hard_exp, axis=1, keepdims=True)
    rows = q_ref.shape[0]
    eye = lax.broadcasted_iota(jnp.int32, (rows, rows), 0) == lax.broadcasted_iota(jnp.int32, (rows, rows), 1)
    positive = left_index == column_ref[...].astype(jnp.int32)
    chosen = jnp.sum(jnp.where(positive, logits, 0.0), axis=1, keepdims=True)
    loss = jnp.log(denominator) + peak - chosen
    loss_ref[...] = jnp.sum(jnp.where(eye, loss, 0.0), axis=0, keepdims=True)
    weights = (cycle_exp / denominator - jnp.where(positive, 1.0, 0.0)).astype(jnp.bfloat16)
    hard_weights = (hard_exp / denominator).astype(jnp.bfloat16)
    right_weights = dots(weights, order).astype(jnp.bfloat16)

    copies = []
    for start, w, rows_ref in ((0, weights, left_ref), (half, right_weights, right_ref)):
        all_weights = jnp.concatenate([w, hard_weights], axis=1)
        for chunk in range(0, half, 512):
            at = slice(start + chunk, start + chunk + 512)
            all_rows = [rows_ref[:, chunk : chunk + 512]] + [pool[:, at] for pool in (p0, p1, p2, p3)]
            grad = jnp.dot(all_weights, jnp.concatenate(all_rows, axis=0), preferred_element_type=jnp.float32)
            out_ref[:, at] = grad.astype(jnp.bfloat16)
            copy = pltpu.make_async_copy(out_ref.at[:, at], grad_ref.at[:, at], sems.at[len(copies)])
            copy.start()
            copies.append(copy)
    for copy in copies:
        copy.wait()


VMEM = functools.partial(pl.BlockSpec, memory_space=pltpu.VMEM)
SMEM = functools.partial(pl.BlockSpec, memory_space=pltpu.SMEM)


def small_call(kernel, outs, args, name, scalars=0, flops=2**33):
    return pl.pallas_call(
        kernel,
        out_shape=outs,
        in_specs=[SMEM()] * scalars + [VMEM()] * (len(args) - scalars),
        out_specs=jax.tree.map(lambda _: VMEM(), outs),
        compiler_params=pltpu.CompilerParams(vmem_limit_bytes=8 * 2**20),
        cost_estimate=pl.CostEstimate(flops=flops, bytes_accessed=4 * 2**20, transcendentals=0),
        name=name,
    )(*args)


def mask_call(place, refs, count, lists):
    rows = refs.shape[0]
    out = jax.ShapeDtypeStruct((rows, 4 * lists.size), jnp.float32)
    return small_call(mask_kernel, out, (place, refs.T, count.reshape(1, rows), lists[0]), "mask", scalars=1)


def hard_call(place, positive, mask, queries, pools):
    rows = queries.shape[0]
    out = jax.ShapeDtypeStruct(mask.shape, mask.dtype)
    order = jax.ShapeDtypeStruct((8 * BLOCK, 8 * BLOCK), jnp.bfloat16)
    column = jax.ShapeDtypeStruct((rows, 1), jnp.float32)
    args = (place, positive.reshape(1, rows), mask, queries, *pools)
    return small_call(hard_kernel, (out, order, column), args, "hard", scalars=1, flops=2**34)


def copies_call(passages):
    rows, width = passages.shape
    out = jax.ShapeDtypeStruct((8, rows, width // 2), passages.dtype)
    return small_call(copies_kernel, out, (passages,), "copies", flops=2**20)


def sort_call(place, mine, theirs):
    out = jax.ShapeDtypeStruct((2, BLOCK, mine.shape[2]), mine.dtype)
    return small_call(sort_kernel, (out, out, out), (place, mine, theirs), "sort", scalars=1)


def hand_call(left, right, *waiting, flops=2**33):
    one = jax.ShapeDtypeStruct((1,) + left.shape[1:], left.dtype)
    out = jax.ShapeDtypeStruct((2 + sum(part.shape[0] for part in waiting),) + left.shape[1:], left.dtype)
    return small_call(hand_kernel, (one, one, out), (left, right, *waiting), "hand", flops=flops)


def tail_call(place, column, hard, order, queries, blocks, pools):
    rows, width = queries.shape
    half = width // 2
    return pl.pallas_call(
        tail_kernel,
        out_shape=(
            jax.ShapeDtypeStruct((rows, width), jnp.bfloat16),
            jax.ShapeDtypeStruct((1, rows), jnp.float32),
        ),
        in_specs=[SMEM()] + [VMEM()] * (4 + len(blocks) + len(pools)),
        out_specs=(pl.BlockSpec(memory_space=pl.ANY), VMEM()),
        scratch_shapes=[
            pltpu.VMEM((8 * BLOCK, half), jnp.bfloat16),
            pltpu.VMEM((8 * BLOCK, half), jnp.bfloat16),
            pltpu.VMEM((rows, width), jnp.bfloat16),
            pltpu.SemaphoreType.DMA((8,)),
        ],
        compiler_params=pltpu.CompilerParams(vmem_limit_bytes=16 * 2**20),
        cost_estimate=pl.CostEstimate(flops=2**31, bytes_accessed=12 * 2**20, transcendentals=2**17),
        name="tail",
    )(place, column, hard, order, queries, *blocks, *pools)


def body(queries, passages, pool, positive_ids, request_lists, hard_refs, hard_count):
    half = passages.shape[1] // 2
    device = lax.axis_index("d")
    core = device & 1
    place = jnp.stack([device >> 7, (device >> 2) & 7, core, device & 3]).astype(jnp.int32)

    with jax.named_scope("cross"):
        got = lax.all_to_all(copies_call(passages), "d", 0, 0, axis_index_groups=CROSS, tiled=True)
    with jax.named_scope("used"):
        mask = mask_call(place, hard_refs, hard_count, request_lists)
    got, mask = lax.optimization_barrier((got, mask))
    with jax.named_scope("near"):
        got = got.reshape(4, 2, 2, half).transpose(1, 0, 2, 3).reshape(1, 16, half)
        sent = jnp.broadcast_to(got, (8, 16, half))
        near = lax.all_to_all(sent, "d", 0, 0, axis_index_groups=NEAR, tiled=True)
        theirs = lax.ppermute(near, "d", OTHER_CORE)
        left, right, keep = sort_call(place, near, theirs)
    with jax.named_scope("pool_x"):
        near, pool = lax.optimization_barrier((near, pool))
        pool_x = lax.ppermute(pool, "d", OTHER_CHIP)
    with jax.named_scope("ring"):
        blocks = [keep]
        left, right = lax.ppermute(left, "d", RING_Z), lax.ppermute(right, "d", RING_Y)
        pool_c = lax.ppermute(pool, "d", OTHER_CORE)
        for step in range(3):
            waiting = ()
            if step < 2:
                next_left, next_right = lax.ppermute(left, "d", RING_Z), lax.ppermute(right, "d", RING_Y)
            else:
                _, pool_x = lax.optimization_barrier((left, pool_x))
                left, right, *blocks = lax.optimization_barrier((left, right, *blocks))
                waiting = (give,)
            if step == 0:
                left, pool_c = lax.optimization_barrier((left, pool_c))
            keep_left, keep_right, give = hand_call(left, right, *waiting, flops=2**33 if step < 2 else 2**35)
            blocks += [keep_left, keep_right]
            if step == 1:
                last = [lax.ppermute(keep_left, "d", RING_Z2), lax.ppermute(keep_right, "d", RING_Y2)]
            else:
                blocks.append(lax.ppermute(give, "d", OTHER_CORE))
            left, right = next_left, next_right
    with jax.named_scope("other_pools"):
        pool_xc = lax.ppermute(pool_x, "d", OTHER_CORE)
        pools = (pool, pool_c, pool_x, pool_xc)
        hard, order, column = hard_call(place, positive_ids, mask, queries, pools)
    grad, loss = tail_call(place, column, hard, order, queries, blocks + last, pools)
    return grad, loss.reshape(-1)


def solution(mesh):
    flat = Mesh(mesh.devices.reshape(1024), ("d",))
    return jax.shard_map(
        body,
        mesh=flat,
        in_specs=(P("d", None), P("d", None), P("d", None), P("d"), P("d", None, None), P("d", None), P("d")),
        out_specs=(P("d", None), P("d")),
        check_vma=False,
    )
```
